32 devices in a mesh: groups: 2 (over x), seq: 16 (over z, y, core).
Axes of the slice: x: 2, y: 2, z: 4, core: 2. Of those that a mesh axis runs over, the one named last changes fastest.
Arguments:
- inputs: bfloat16 [8192, 1536], P(('groups', 'seq')), parts along dimension 0, may hold values from -6 to 6
- norm_gain: float32 [1536], replicated, may hold values from 0.1 to 1.9
- dilated_weight: bfloat16 [3, 1536, 768], P(None, 'seq'), may hold values from -0.09375 to 0.09375
- point_weight: bfloat16 [768, 1536], replicated, may hold values from -0.21875 to 0.21875
- cotangent: bfloat16 [8192, 1536], P(('groups', 'seq')), parts along dimension 0, may hold values from -6 to 6
Outputs:
- outputs: bfloat16 [8192, 1536], P(('groups', 'seq')), parts along dimension 0
- input_grad: bfloat16 [8192, 1536], P(('groups', 'seq')), parts along dimension 0
- dilated_grad: float32 [6, 1536, 768], P('groups', 'seq'), parts along dimension 0
- point_grad: float32 [1536, 1536], P('groups', 'seq'), parts along dimension 0
The draws below stay inside these ranges and needn't reach their ends.
There are 2 independent parts, one for each index of `groups`. The reference program is written for one: setup_inputs(seed, part) draws one part's arguments, and reference() takes and returns one part's arrays. A program takes and returns all parts, laid end to end along the dimension named above; an argument that names none is the same for every part. Nothing has to cross between parts.
All inputs are finite; a program needn't handle non-finite values.
Results may differ from the reference program's by a relative error of at most 0.0053.
Values may be sent and summed in bfloat16 or wider, within the bound.
No kernel may reach another device: no remote copies, remote signals or barrier semaphores. Data moves between devices by JAX's collectives and lax.ppermute only.
A program may use at most 128 MiB of HBM per device.

```python
import math
import jax
import jax.numpy as jnp
from jax import lax

C = 1536
H = 768
POS_DEV = 256
HOPS = 1
LEN = 4096


def raised(entries, rng, source, target, blocks, factor):
    def block_of(dim):
        return (jnp.arange(entries.shape[dim]) // (entries.shape[dim] // blocks)).reshape((-1,) + (1,) * (entries.ndim - 1 - dim))

    near = jax.random.permutation(rng, blocks)[block_of(target)]
    second = (block_of(target) + blocks // 2) % blocks
    return jnp.where((block_of(source) == near) | (block_of(source) == second), factor * entries, entries)


def shard_levels(own_key, dims, shards, low, high):
    factor_of = 1.0
    for dim, parts in shards:
        draws = jax.random.uniform(jax.random.fold_in(jax.random.fold_in(own_key, 6), dim), (parts,), jnp.float32, low / len(shards), high / len(shards))
        factor_of = factor_of * jnp.repeat(jnp.exp(draws), dims[dim] // parts).reshape((-1,) + (1,) * (len(dims) - 1 - dim))
    return factor_of


def scatter_about(rng, dims, width, bound, pieces=(), held_as=jnp.bfloat16):
    factor_of = shard_levels(rng, dims, pieces, -0.22, 0.18) if pieces else 1.0
    result = jax.random.normal(rng, dims, jnp.float32) * width * factor_of
    return jnp.minimum(jnp.maximum(result, -bound), bound).astype(held_as)


def noise_with(key, dims, deviation, reach, shards, heavy, kind=jnp.bfloat16):
    values = deviation * jax.random.normal(key, dims, jnp.float32)
    if shards:
        values = values * shard_levels(key, dims, shards, -0.22, 0.18)
    return jnp.clip(raised(values, jax.random.fold_in(key, 3), *heavy), -reach, reach).astype(kind)


def setup_inputs(seed: int = 0, part: int = 0) -> dict:
    key_list = jax.random.split(jax.random.key(seed), 6)
    part_splits = jax.random.split(jax.random.fold_in(key_list[5], part), 6)
    inputs = noise_with(part_splits[0], (LEN, C), 1.0, 6.0, ((0, 16),), (0, 1, 16, 2.0))
    norm_gain = jnp.clip(1.0 + 0.18 * jax.random.normal(key_list[1], (C,), jnp.float32), 0.1, 1.9)
    dilated_weight = scatter_about(key_list[2], (3, C, H), (3 * C) ** -0.5, 0.09375, ((1, 16),))
    point_weight = scatter_about(key_list[3], (H, C), H ** -0.5, 0.21875)
    cotangent = noise_with(part_splits[4], (LEN, C), 1.0, 6.0, ((0, 16),), (0, 1, 16, 2.0))
    return dict(inputs=inputs, norm_gain=norm_gain, dilated_weight=dilated_weight, point_weight=point_weight, cotangent=cotangent)


root_coef = math.sqrt(2.0 / math.pi)

def gelu_value(v):
    return 0.5 * v * (1.0 + jnp.tanh(root_coef * (v + 0.044715 * v * v * v)))

def gelu_slope(v):
    inner = jnp.tanh(root_coef * (v + 0.044715 * v * v * v))
    return 0.5 * (1.0 + inner) + 0.5 * v * (1.0 - inner * inner) * root_coef * (1.0 + 3.0 * 0.044715 * v * v)

def shift_rows(values, offset):
    if offset == 0:
        return values
    blank = jnp.zeros((abs(offset), values.shape[1]), values.dtype)
    if offset > 0:
        return jnp.concatenate([values[offset:], blank], axis=0)
    return jnp.concatenate([blank, values[:offset]], axis=0)

def reference(inputs, norm_gain, dilated_weight, point_weight, cotangent):
    dilation = HOPS * POS_DEV
    xfull = inputs.astype(jnp.float32)
    ratio = lax.rsqrt(lax.optimization_barrier(jnp.mean(xfull * xfull, axis=-1, keepdims=True)) + 1e-06)
    normed = xfull * ratio * norm_gain
    act = gelu_value(normed).astype(jnp.bfloat16)
    shifted = [shift_rows(act, (k - 1) * dilation) for k in range(3)]
    pre = jnp.zeros((act.shape[0], dilated_weight.shape[2]), jnp.float32)
    for k in range(3):
        pre = pre + jnp.dot(shifted[k], dilated_weight[k], preferred_element_type=jnp.float32)
    branch = gelu_value(pre).astype(jnp.bfloat16)
    outputs = (xfull + jnp.dot(branch, point_weight, preferred_element_type=jnp.float32)).astype(jnp.bfloat16)
    branch_grad = lax.dot_general(cotangent, point_weight, (((1,), (1,)), ((), ())), preferred_element_type=jnp.float32)
    pre_grad = (branch_grad * gelu_slope(pre)).astype(jnp.bfloat16)
    point_grad = lax.dot_general(branch, cotangent, (((0,), (0,)), ((), ())), preferred_element_type=jnp.float32)
    dilated_grad = jnp.stack([lax.dot_general(shifted[k], pre_grad, (((0,), (0,)), ((), ())), preferred_element_type=jnp.float32) for k in range(3)])
    act_grad = jnp.zeros(act.shape, jnp.float32)
    for k in range(3):
        moved = shift_rows(pre_grad, -(k - 1) * dilation)
        act_grad = act_grad + lax.dot_general(moved, dilated_weight[k], (((1,), (1,)), ((), ())), preferred_element_type=jnp.float32)
    scaled = act_grad * gelu_slope(normed) * norm_gain
    inner = lax.optimization_barrier(jnp.mean(scaled * xfull, axis=-1, keepdims=True))
    input_grad = (cotangent.astype(jnp.float32) + ratio * scaled - xfull * ratio * ratio * ratio * inner).astype(jnp.bfloat16)
    return (outputs, input_grad, dilated_grad, point_grad)
```

```python
import math

import jax
import jax.numpy as jnp
from jax import lax
from jax.sharding import PartitionSpec as P

root_coef = math.sqrt(2.0 / math.pi)
bf16 = jnp.bfloat16
f32 = jnp.float32


def gelu_value(v):
    return 0.5 * v * (1.0 + jnp.tanh(root_coef * (v + 0.044715 * v * v * v)))


def gelu_slope(v):
    inner = jnp.tanh(root_coef * (v + 0.044715 * v * v * v))
    return 0.5 * (1.0 + inner) + 0.5 * v * (1.0 - inner * inner) * root_coef * (
        1.0 + 3.0 * 0.044715 * v * v
    )


def product(left, right):
    return jnp.dot(left, right, preferred_element_type=f32)


def transposed_product(left, weight):
    return lax.dot_general(
        left, weight, (((1,), (1,)), ((), ())), preferred_element_type=f32
    )


def in_order(first, mine, other, axis):
    return jnp.where(
        first,
        jnp.concatenate([mine, other], axis),
        jnp.concatenate([other, mine], axis),
    )


def local(inputs, norm_gain, dilated_weight, point_weight, cotangent):
    size = lax.axis_size("seq")
    depth = size // 4
    me = lax.axis_index("seq")
    core = me % 2
    y = (me // 2) % 2
    z = me // 4
    rows, channels = inputs.shape
    own = dilated_weight.shape[1]
    hidden = dilated_weight.shape[2]
    half = hidden // 2
    block = 2 * own

    def send(value, target):
        pairs = [(i, target(i)) for i in range(size)]
        return lax.ppermute(value, "seq", [p for p in pairs if 0 <= p[1] < size])

    def to_core(value):
        return send(value, lambda i: i ^ 1)

    def to_y(value):
        return send(value, lambda i: i ^ 2)

    def to_z(value, by):
        return send(value, lambda i: (i + 4 * by) % size)

    def cut(value, start, length, axis):
        return lax.dynamic_slice_in_dim(value, start, length, axis)

    mine = cut(dilated_weight, core * half, half, 2)
    theirs = cut(dilated_weight, (1 - core) * half, half, 2)
    chip_taps = in_order(core == 0, mine, to_core(theirs), 1)
    columns = [chip_taps] + [to_z(chip_taps, d) for d in range(1, depth)]
    beside = [to_y(c) for c in columns]
    taps = jnp.zeros((3, channels, half), bf16)
    for d in range(depth):
        source = (z - d) % depth
        taps = lax.dynamic_update_slice_in_dim(
            taps, columns[d], (source * 2 + y) * block, 1
        )
        taps = lax.dynamic_update_slice_in_dim(
            taps, beside[d], (source * 2 + 1 - y) * block, 1
        )

    xfull = inputs.astype(f32)
    ratio = lax.rsqrt(jnp.mean(xfull * xfull, axis=-1, keepdims=True) + 1e-06)
    normed = xfull * ratio * norm_gain
    act = gelu_value(normed).astype(bf16)
    edge = send(act, lambda i: i + 1 if i % 2 else i - 1)
    act_inner = in_order(core == 0, act, to_core(act), 0)
    edge_other = to_core(edge)
    low = jnp.where(core == 0, edge, edge_other)
    high = jnp.where(core == 0, edge_other, edge)
    act_wide = jnp.concatenate([low, act_inner, high], 0)

    cot = in_order(core == 0, cotangent, to_core(cotangent), 0)
    point_rows = cut(point_weight, core * half, half, 0)
    branch_grad = transposed_product(cot, point_rows)

    act_turned = act_wide.T.reshape(depth, 2, block, 4 * rows)
    far_part = lax.dynamic_slice(
        act_turned,
        (0, 1 - y, 0, (y * 2 + core) * rows),
        (depth, 1, block, rows),
    ).reshape(depth * block, rows)
    far = to_y(far_part)
    far = in_order(core == 0, far, to_core(far), 1)
    near = cut(act_turned, y, 1, 1).reshape(depth * block, 4 * rows)
    act_row = in_order(y == 0, near, far, 1)

    pre = product(act_wide[: 2 * rows], taps[0])
    pre = pre + product(act_wide[rows : 3 * rows], taps[1])
    pre = pre + product(act_wide[2 * rows :], taps[2])
    branch = gelu_value(pre).astype(bf16)
    pre_grad = (branch_grad * gelu_slope(pre)).astype(bf16)

    grad_row = in_order(y == 0, pre_grad, to_y(pre_grad), 0)
    grad_low = send(pre_grad[rows:], lambda i: i + 2)
    grad_high = send(pre_grad[:rows], lambda i: i - 2)

    def spread(partial):
        total = lax.dynamic_index_in_dim(partial, z, 0, keepdims=False)
        for d in range(1, depth):
            piece = lax.dynamic_index_in_dim(
                partial, (z + d) % depth, 0, keepdims=False
            )
            total = total + to_z(piece.astype(bf16), d).astype(f32)
        return total

    tap_terms = jnp.stack(
        [
            product(act_row[:, k * rows : (k + 4) * rows], grad_row).reshape(
                depth, block, half
            )
            for k in range(3)
        ],
        1,
    )
    tap_sum = spread(tap_terms)

    cot_turned = cot.T.reshape(depth, 2, block, 2 * rows)

    def point_term(parity):
        picked = cut(cot_turned, parity, 1, 1).reshape(depth * block, 2 * rows)
        return product(picked, branch).reshape(depth, block, half)

    point_terms = point_term(y) + to_y(point_term(1 - y).astype(bf16)).astype(f32)
    point_sum = spread(point_terms)

    branch_other = to_core(cut(branch, (1 - core) * rows, rows, 0))
    branch_own = in_order(
        core == 0, cut(branch, core * rows, rows, 0), branch_other, 1
    )
    outputs = (xfull + product(branch_own, point_weight)).astype(bf16)

    grad_wide = jnp.concatenate([grad_low, pre_grad, grad_high], 0)
    act_grad = transposed_product(grad_wide[2 * rows :], taps[0])
    act_grad = act_grad + transposed_product(grad_wide[rows : 3 * rows], taps[1])
    act_grad = act_grad + transposed_product(grad_wide[: 2 * rows], taps[2])
    act_grad = cut(act_grad, core * rows, rows, 0) + to_core(
        cut(act_grad, (1 - core) * rows, rows, 0)
    )
    scaled = act_grad * gelu_slope(normed) * norm_gain
    inner = jnp.mean(scaled * xfull, axis=-1, keepdims=True)
    input_grad = (
        cotangent.astype(f32) + ratio * scaled - xfull * ratio * ratio * ratio * inner
    ).astype(bf16)

    sums = jnp.concatenate([tap_sum, point_sum[None]], 0)
    sums = in_order(
        core == 0,
        cut(sums, core * own, own, 1),
        to_core(cut(sums, (1 - core) * own, own, 1)),
        2,
    )
    return (outputs, input_grad, sums[:3], sums[3].T)


def solution(mesh):
    placed = (
        P(("groups", "seq"), None),
        P(),
        P(None, "seq", None),
        P(),
        P(("groups", "seq"), None),
    )
    return jax.shard_map(
        local,
        mesh=mesh,
        in_specs=placed,
        out_specs=(
            P(("groups", "seq"), None),
            P(("groups", "seq"), None),
            P("groups", "seq", None),
            P("groups", "seq"),
        ),
        check_vma=False,
    )
```

```python
import functools
import math

import jax
import jax.numpy as jnp
from jax import lax
from jax.experimental import pallas as pl
from jax.experimental.pallas import tpu as pltpu
from jax.sharding import PartitionSpec as P

root_coef = math.sqrt(2.0 / math.pi)
bf16 = jnp.bfloat16
f32 = jnp.float32


def gelu_value(v):
    return 0.5 * v * (1.0 + jnp.tanh(root_coef * (v + 0.044715 * v * v * v)))


def gelu_slope(v):
    inner = jnp.tanh(root_coef * (v + 0.044715 * v * v * v))
    return 0.5 * (1.0 + inner) + 0.5 * v * (1.0 - inner * inner) * root_coef * (
        1.0 + 3.0 * 0.044715 * v * v
    )


def product(left, right):
    return jnp.dot(left, right, preferred_element_type=f32)


def transposed_product(left, weight):
    return lax.dot_general(
        left, weight, (((1,), (1,)), ((), ())), preferred_element_type=f32
    )


def in_order(first, mine, other, axis):
    return jnp.where(
        first,
        jnp.concatenate([mine, other], axis),
        jnp.concatenate([other, mine], axis),
    )


MIB = 1024 * 1024


def position():
    me = lax.axis_index("seq")
    return me // 4, (me // 2) % 2, me % 2


def fetch(pairs, sems):
    copies = [
        pltpu.make_async_copy(src, dst, sems.at[i]) for i, (src, dst) in enumerate(pairs)
    ]
    for copy in copies:
        copy.start()
    for copy in copies:
        copy.wait()


def tap_copies(pieces, whole):
    z, y, _ = position()
    depth = len(pieces) // 2
    block = pieces[0].shape[1]
    pairs = []
    for i, piece in enumerate(pieces):
        source = lax.rem(z + depth - i % depth, depth)
        side = y if i < depth else 1 - y
        start = pl.multiple_of((source * 2 + side) * block, block)
        pairs.append((piece, whole.at[:, pl.ds(start, block), :]))
    return pairs


def forward_kernel(count, *refs):
    pieces = refs[:count]
    act, act_other, edge, edge_other, slope_in = refs[count : count + 5]
    branch, grad, wide, taps, sems = refs[count + 5 :]
    _, _, core = position()
    rows = act.shape[0]

    def at(start):
        return wide.at[pl.ds(pl.multiple_of(start * rows, rows), rows), :]

    fetch(
        [
            (act, at(1 + core)),
            (act_other, at(2 - core)),
            (edge, at(3 * core)),
            (edge_other, at(3 - 3 * core)),
        ]
        + tap_copies(pieces, taps),
        sems,
    )
    for part in range(2):
        pre = product(wide[pl.ds(part * rows, rows), :], taps[0])
        pre = pre + product(wide[pl.ds((part + 1) * rows, rows), :], taps[1])
        pre = pre + product(wide[pl.ds((part + 2) * rows, rows), :], taps[2])
        here = pl.ds(part * rows, rows)
        branch[here, :] = gelu_value(pre).astype(bf16)
        grad[here, :] = (slope_in[here, :] * gelu_slope(pre)).astype(bf16)


def terms_kernel(depth, near, far, far_other, mine, other, *refs):
    outs = refs[:depth]
    wide, grads, sems = refs[depth:]
    z, y, core = position()
    rows = far.shape[-1]
    span = mine.shape[0]

    def at(start):
        return wide.at[:, :, pl.ds(pl.multiple_of(start * rows, rows), rows)]

    fetch(
        [
            (
                near.at[:, y],
                wide.at[:, :, pl.ds(pl.multiple_of(y * 2 * rows, 2 * rows), 4 * rows)],
            ),
            (far, at((1 - y) * 4 + core)),
            (far_other, at((1 - y) * 4 + 1 - core)),
            (mine, grads.at[pl.ds(pl.multiple_of(y * span, span), span), :]),
            (other, grads.at[pl.ds(pl.multiple_of((1 - y) * span, span), span), :]),
        ],
        sems,
    )
    for i in range(depth):
        d = (i + 1) % depth
        target = lax.rem(z + d, depth)
        for k in range(3):
            outs[d][k] = product(
                wide[target, :, pl.ds(k * rows, 4 * rows)], grads[...]
            ).astype(outs[d].dtype)


def point_kernel(depth, turned, branch, *outs):
    z, _, _ = position()
    for i in range(depth):
        d = (i + 1) % depth
        target = lax.rem(z + d, depth)
        outs[d][...] = product(turned[target], branch[...]).astype(outs[d].dtype)


def backward_kernel(count, *refs):
    pieces = refs[:count]
    low, grad, high = refs[count : count + 3]
    mine, other, wide, taps, sems = refs[count + 3 :]
    _, _, core = position()
    rows = low.shape[0]
    fetch(
        [
            (low, wide.at[pl.ds(0, rows), :]),
            (grad, wide.at[pl.ds(rows, 2 * rows), :]),
            (high, wide.at[pl.ds(3 * rows, rows), :]),
        ]
        + tap_copies(pieces, taps),
        sems,
    )
    for out, part in ((other, 1 - core), (mine, core)):
        total = None
        for k in range(3):
            start = pl.multiple_of((part + 2 - k) * rows, rows)
            term = transposed_product(wide[pl.ds(start, rows), :], taps[k])
            total = term if total is None else total + term
        out[...] = total


def call(kernel, outs, args, specs, scratch, flops, limit):
    nbytes = sum(a.size * a.dtype.itemsize for a in args) + sum(
        math.prod(s) * jnp.dtype(t).itemsize for s, t in outs
    )
    return pl.pallas_call(
        kernel,
        out_shape=[jax.ShapeDtypeStruct(s, t) for s, t in outs],
        in_specs=[pl.BlockSpec(memory_space=m) for m in specs],
        out_specs=[pl.BlockSpec(memory_space=pltpu.VMEM)] * len(outs),
        scratch_shapes=scratch,
        compiler_params=pltpu.CompilerParams(vmem_limit_bytes=limit * MIB),
        cost_estimate=pl.CostEstimate(
            flops=flops, bytes_accessed=nbytes, transcendentals=0
        ),
    )(*args)


def local(inputs, norm_gain, dilated_weight, point_weight, cotangent):
    size = lax.axis_size("seq")
    depth = size // 4
    z, y, core = position()
    rows, channels = inputs.shape
    own = dilated_weight.shape[1]
    hidden = dilated_weight.shape[2]
    half = hidden // 2
    block = 2 * own
    span = 2 * rows

    def send(value, target):
        pairs = [(i, target(i)) for i in range(size)]
        return lax.ppermute(value, "seq", [p for p in pairs if 0 <= p[1] < size])

    def to_core(value):
        return send(value, lambda i: i ^ 1)

    def to_y(value):
        return send(value, lambda i: i ^ 2)

    def to_z(value, by):
        return send(value, lambda i: (i + 4 * by) % size)

    def cut(value, start, length, axis):
        return lax.dynamic_slice_in_dim(value, start, length, axis)

    mine = cut(dilated_weight, core * half, half, 2)
    theirs = cut(dilated_weight, (1 - core) * half, half, 2)
    chip_taps = in_order(core == 0, mine, to_core(theirs), 1)
    pieces = [chip_taps] + [to_z(chip_taps, d) for d in range(1, depth)]
    pieces = pieces + [to_y(c) for c in pieces]

    xfull = inputs.astype(f32)
    ratio = lax.rsqrt(jnp.mean(xfull * xfull, axis=-1, keepdims=True) + 1e-06)
    normed = xfull * ratio * norm_gain
    act = gelu_value(normed).astype(bf16)
    edge = send(act, lambda i: i + 1 if i % 2 else i - 1)
    act_other = to_core(act)
    edge_other = to_core(edge)

    cot_other = to_core(cotangent)
    cot = in_order(core == 0, cotangent, cot_other, 0)
    point_rows = cut(point_weight, core * half, half, 0)
    branch_grad = transposed_product(cot, point_rows)
    cot_turned = cot.T.reshape(depth, 2 * block, span)

    act_wide = jnp.concatenate(
        [
            jnp.where(core == 0, edge, edge_other),
            in_order(core == 0, act, act_other, 0),
            jnp.where(core == 0, edge_other, edge),
        ],
        0,
    )
    act_turned = act_wide.T.reshape(depth, 2, block, 4 * rows)
    far = to_y(
        lax.dynamic_slice(
            act_turned,
            (0, 1 - y, 0, (y * 2 + core) * rows),
            (depth, 1, block, rows),
        ).reshape(depth, block, rows)
    )
    far_other = to_core(far)

    count = len(pieces)
    branch, pre_grad = call(
        functools.partial(forward_kernel, count),
        [((span, half), bf16)] * 2,
        [*pieces, act, act_other, edge, edge_other, branch_grad],
        [pl.ANY] * (count + 4) + [pltpu.VMEM],
        [
            pltpu.VMEM((4 * rows, channels), bf16),
            pltpu.VMEM((3, channels, half), bf16),
            pltpu.SemaphoreType.DMA((count + 4,)),
        ],
        6 * span * channels * half,
        24,
    )

    grad_far = to_y(pre_grad)
    grad_low = send(pre_grad[rows:], lambda i: i + 2)
    grad_high = send(pre_grad[:rows], lambda i: i - 2)

    def gathered(terms):
        total = terms[0]
        for d in range(1, depth):
            total = total + to_z(terms[d], d).astype(f32)
        return total

    point_terms = call(
        functools.partial(point_kernel, depth),
        [((2 * block, half), bf16 if d else f32) for d in range(depth)],
        [cot_turned, branch],
        [pltpu.VMEM] * 2,
        [],
        2 * span * channels * half,
        16,
    )
    point_sum = gathered(point_terms)

    tap_terms = call(
        functools.partial(terms_kernel, depth),
        [((3, block, half), bf16 if d else f32) for d in range(depth)],
        [act_turned, far, far_other, pre_grad, grad_far],
        [pl.ANY] * 5,
        [
            pltpu.VMEM((depth, block, 6 * rows), bf16),
            pltpu.VMEM((2 * span, half), bf16),
            pltpu.SemaphoreType.DMA((5,)),
        ],
        6 * span * channels * half,
        24,
    )
    tap_sum = gathered(tap_terms)

    point_sum = cut(point_sum, y * block, block, 0) + to_y(
        cut(point_sum, (1 - y) * block, block, 0).astype(bf16)
    ).astype(f32)

    branch_other = to_core(cut(branch, (1 - core) * rows, rows, 0))
    branch_own = in_order(
        core == 0, cut(branch, core * rows, rows, 0), branch_other, 1
    )
    outputs = (xfull + product(branch_own, point_weight)).astype(bf16)

    act_grad, act_grad_other = call(
        functools.partial(backward_kernel, count),
        [((rows, channels), f32)] * 2,
        [*pieces, grad_low, pre_grad, grad_high],
        [pl.ANY] * (count + 3),
        [
            pltpu.VMEM((4 * rows, half), bf16),
            pltpu.VMEM((3, channels, half), bf16),
            pltpu.SemaphoreType.DMA((count + 3,)),
        ],
        6 * span * channels * half,
        24,
    )
    act_grad = act_grad + to_core(act_grad_other)
    scaled = act_grad * gelu_slope(normed) * norm_gain
    inner = jnp.mean(scaled * xfull, axis=-1, keepdims=True)
    input_grad = (
        cotangent.astype(f32) + ratio * scaled - xfull * ratio * ratio * ratio * inner
    ).astype(bf16)

    sums = jnp.concatenate([tap_sum, point_sum[None]], 0)
    sums = in_order(
        core == 0,
        cut(sums, core * own, own, 1),
        to_core(cut(sums, (1 - core) * own, own, 1)),
        2,
    )
    return (outputs, input_grad, sums[:3], sums[3].T)


def solution(mesh):
    placed = (
        P(("groups", "seq"), None),
        P(),
        P(None, "seq", None),
        P(),
        P(("groups", "seq"), None),
    )
    return jax.shard_map(
        local,
        mesh=mesh,
        in_specs=placed,
        out_specs=(
            P(("groups", "seq"), None),
            P(("groups", "seq"), None),
            P("groups", "seq", None),
            P("groups", "seq"),
        ),
        check_vma=False,
    )
```

```python
import functools
import math

import jax
import jax.numpy as jnp
from jax import lax
from jax.experimental import pallas as pl
from jax.experimental.pallas import tpu as pltpu
from jax.sharding import PartitionSpec as P

root_coef = math.sqrt(2.0 / math.pi)
bf16 = jnp.bfloat16
f32 = jnp.float32


def gelu_value(v):
    return 0.5 * v * (1.0 + jnp.tanh(root_coef * (v + 0.044715 * v * v * v)))


def gelu_slope(v):
    inner = jnp.tanh(root_coef * (v + 0.044715 * v * v * v))
    return 0.5 * (1.0 + inner) + 0.5 * v * (1.0 - inner * inner) * root_coef * (
        1.0 + 3.0 * 0.044715 * v * v
    )


def after(value, *others):
    return lax.optimization_barrier((value, *others))[0]


def product(left, right):
    return jnp.dot(left, right, preferred_element_type=f32)


def transposed_product(left, weight):
    return lax.dot_general(
        left, weight, (((1,), (1,)), ((), ())), preferred_element_type=f32
    )


def in_order(first, mine, other, axis):
    return jnp.where(
        first,
        jnp.concatenate([mine, other], axis),
        jnp.concatenate([other, mine], axis),
    )


MIB = 1024 * 1024


def position():
    me = lax.axis_index("seq")
    return me // 4, (me // 2) % 2, me % 2


def fetch(pairs, sems):
    copies = [
        pltpu.make_async_copy(src, dst, sems.at[i]) for i, (src, dst) in enumerate(pairs)
    ]
    for copy in copies:
        copy.start()
    for copy in copies:
        copy.wait()


def tap_copies(places, pieces, whole):
    z, y, _ = position()
    parity = lax.rem(lax.axis_index("groups"), 2)
    pairs = []
    for (shift, across, part), piece in zip(places, pieces):
        size = piece.shape[1]
        depth = lax.axis_size("seq") // 4
        source = lax.rem(z + depth - shift, depth)
        side = 1 - y if across else y
        start = source * 2 + side
        if part is not None:
            start = start * 2 + (1 - parity if part else parity)
        start = pl.multiple_of(start * size, size)
        pairs.append((piece, whole.at[:, pl.ds(start, size), :]))
    return pairs


def forward_kernel(places, *refs):
    count = len(places)
    pieces = refs[:count]
    act, act_other, edge, edge_other, slope_in = refs[count : count + 5]
    branch, grad, wide, taps, sems = refs[count + 5 :]
    _, _, core = position()
    rows = act.shape[0]

    def at(start):
        return wide.at[pl.ds(pl.multiple_of(start * rows, rows), rows), :]

    fetch(
        [
            (act, at(1 + core)),
            (act_other, at(2 - core)),
            (edge, at(3 * core)),
            (edge_other, at(3 - 3 * core)),
        ]
        + tap_copies(places, pieces, taps),
        sems,
    )
    for part in range(2):
        pre = product(wide[pl.ds(part * rows, rows), :], taps[0])
        pre = pre + product(wide[pl.ds((part + 1) * rows, rows), :], taps[1])
        pre = pre + product(wide[pl.ds((part + 2) * rows, rows), :], taps[2])
        here = pl.ds(part * rows, rows)
        branch[here, :] = gelu_value(pre).astype(bf16)
        grad[here, :] = (slope_in[here, :] * gelu_slope(pre)).astype(bf16)


def terms_kernel(depth, near, far, far_other, mine, other, *refs):
    outs = refs[:depth]
    wide, grads, sems = refs[depth:]
    z, y, core = position()
    rows = far.shape[-1]
    span = mine.shape[0]

    def at(start):
        return wide.at[:, :, pl.ds(pl.multiple_of(start * rows, rows), rows)]

    fetch(
        [
            (
                near.at[:, y],
                wide.at[:, :, pl.ds(pl.multiple_of(y * 2 * rows, 2 * rows), 4 * rows)],
            ),
            (far, at((1 - y) * 4 + core)),
            (far_other, at((1 - y) * 4 + 1 - core)),
            (mine, grads.at[pl.ds(pl.multiple_of(y * span, span), span), :]),
            (other, grads.at[pl.ds(pl.multiple_of((1 - y) * span, span), span), :]),
        ],
        sems,
    )
    for i in range(depth):
        d = (i + 1) % depth
        target = lax.rem(z + d, depth)
        for k in range(3):
            outs[d][k] = product(
                wide[target, :, pl.ds(k * rows, 4 * rows)], grads[...]
            ).astype(outs[d].dtype)


def point_kernel(depth, turned, branch, *outs):
    z, _, _ = position()
    for i in range(depth):
        d = (i + 1) % depth
        target = lax.rem(z + d, depth)
        outs[d][...] = product(turned[target], branch[...]).astype(outs[d].dtype)


def backward_kernel(places, *refs):
    count = len(places)
    pieces = refs[:count]
    low, grad, high = refs[count : count + 3]
    mine, other, wide, taps, sems = refs[count + 3 :]
    _, _, core = position()
    rows = low.shape[0]
    fetch(
        [
            (low, wide.at[pl.ds(0, rows), :]),
            (grad, wide.at[pl.ds(rows, 2 * rows), :]),
            (high, wide.at[pl.ds(3 * rows, rows), :]),
        ]
        + tap_copies(places, pieces, taps),
        sems,
    )
    for out, part in ((other, 1 - core), (mine, core)):
        total = None
        for k in range(3):
            start = pl.multiple_of((part + 2 - k) * rows, rows)
            term = transposed_product(wide[pl.ds(start, rows), :], taps[k])
            total = term if total is None else total + term
        out[...] = total


def call(kernel, outs, args, specs, scratch, flops, limit):
    nbytes = sum(a.size * a.dtype.itemsize for a in args) + sum(
        math.prod(s) * jnp.dtype(t).itemsize for s, t in outs
    )
    return pl.pallas_call(
        kernel,
        out_shape=[jax.ShapeDtypeStruct(s, t) for s, t in outs],
        in_specs=[pl.BlockSpec(memory_space=m) for m in specs],
        out_specs=[pl.BlockSpec(memory_space=pltpu.VMEM)] * len(outs),
        scratch_shapes=scratch,
        compiler_params=pltpu.CompilerParams(vmem_limit_bytes=limit * MIB),
        cost_estimate=pl.CostEstimate(
            flops=flops, bytes_accessed=nbytes, transcendentals=0
        ),
    )(*args)


def local(inputs, norm_gain, dilated_weight, point_weight, cotangent):
    size = lax.axis_size("seq")
    depth = size // 4
    z, y, core = position()
    rows, channels = inputs.shape
    own = dilated_weight.shape[1]
    hidden = dilated_weight.shape[2]
    half = hidden // 2
    block = 2 * own
    span = 2 * rows

    def send(value, target):
        pairs = [(i, target(i)) for i in range(size)]
        return lax.ppermute(value, "seq", [p for p in pairs if 0 <= p[1] < size])

    def to_core(value):
        return send(value, lambda i: i ^ 1)

    def to_y(value):
        return send(value, lambda i: i ^ 2)

    def to_z(value, by):
        return send(value, lambda i: (i + 4 * by) % size)

    groups = lax.axis_size("groups")
    halved = groups % 2 == 0 and own % 16 == 0

    def to_x(value):
        return lax.ppermute(value, "groups", [(g, g ^ 1) for g in range(groups)])

    def cut(value, start, length, axis):
        return lax.dynamic_slice_in_dim(value, start, length, axis)

    mine = cut(dilated_weight, core * half, half, 2)
    theirs = cut(dilated_weight, (1 - core) * half, half, 2)
    swapped = to_core(theirs)
    if halved:
        parity = lax.axis_index("groups") % 2
        start_piece = jnp.where(core == parity, mine, swapped)
        rest_piece = jnp.where(core == parity, swapped, mine)
    else:
        start_piece = in_order(core == 0, mine, swapped, 1)
    part = 0 if halved else None
    along = [start_piece] + [to_z(start_piece, d) for d in range(1, depth)]
    beside = [to_y(c) for c in along]
    pieces = along + beside
    places = [(d, False, part) for d in range(depth)]
    places += [(d, True, part) for d in range(depth)]
    if halved:
        pieces = pieces + [rest_piece] + [to_x(c) for c in pieces[1:]]
        places = places + [(d, across, 1) for d, across, _ in places]

    inputs = after(inputs, theirs)
    cotangent = after(cotangent, theirs)
    xfull = inputs.astype(f32)
    ratio = lax.rsqrt(jnp.mean(xfull * xfull, axis=-1, keepdims=True) + 1e-06)
    normed = xfull * ratio * norm_gain
    act = gelu_value(normed).astype(bf16)
    edge = send(act, lambda i: i + 1 if i % 2 else i - 1)
    act_other = to_core(act)
    edge_other = to_core(after(edge, *beside[:2]))

    cot_other = to_core(after(cotangent, start_piece))
    cot = in_order(core == 0, cotangent, cot_other, 0)
    point_rows = cut(point_weight, core * half, half, 0)
    branch_grad = transposed_product(cot, point_rows)
    cot_turned = cot.T.reshape(depth, 2 * block, span)

    act_wide = jnp.concatenate(
        [
            jnp.where(core == 0, edge, edge_other),
            in_order(core == 0, act, act_other, 0),
            jnp.where(core == 0, edge_other, edge),
        ],
        0,
    )
    act_turned = act_wide.T.reshape(depth, 2, block, 4 * rows)
    far = to_y(
        lax.dynamic_slice(
            act_turned,
            (0, 1 - y, 0, (y * 2 + core) * rows),
            (depth, 1, block, rows),
        ).reshape(depth, block, rows)
    )
    branch_grad = after(branch_grad, cot_turned, act_turned)
    far_other = to_core(far)

    count = len(pieces)
    branch, pre_grad = call(
        functools.partial(forward_kernel, places),
        [((span, half), bf16)] * 2,
        [*pieces, act, act_other, edge, edge_other, branch_grad],
        [pl.ANY] * (count + 4) + [pltpu.VMEM],
        [
            pltpu.VMEM((4 * rows, channels), bf16),
            pltpu.VMEM((3, channels, half), bf16),
            pltpu.SemaphoreType.DMA((count + 4,)),
        ],
        6 * span * channels * half,
        24,
    )

    grad_far = to_y(pre_grad)
    grad_edge = after(pre_grad, grad_far)
    grad_low = send(grad_edge[rows:], lambda i: i + 2)
    grad_high = send(grad_edge[:rows], lambda i: i - 2)

    def sent(terms):
        return [terms[0]] + [to_z(terms[d], d) for d in range(1, depth)]

    def added(terms):
        total = terms[0]
        for term in terms[1:]:
            total = total + term.astype(f32)
        return total

    point_terms = call(
        functools.partial(point_kernel, depth),
        [((2 * block, half), bf16 if d else f32) for d in range(depth)],
        [cot_turned, branch],
        [pltpu.VMEM] * 2,
        [],
        2 * span * channels * half,
        16,
    )
    point_parts = sent(point_terms)

    tap_terms = call(
        functools.partial(terms_kernel, depth),
        [((3, block, half), bf16 if d else f32) for d in range(depth)],
        [act_turned, far, far_other, pre_grad, grad_far],
        [pl.ANY] * 5,
        [
            pltpu.VMEM((depth, block, 6 * rows), bf16),
            pltpu.VMEM((2 * span, half), bf16),
            pltpu.SemaphoreType.DMA((5,)),
        ],
        6 * span * channels * half,
        24,
    )
    tap_parts = sent(tap_terms)
    tap_sum = added(tap_parts)

    branch = after(branch, tap_terms[0])
    branch_other = to_core(cut(branch, (1 - core) * rows, rows, 0))
    branch_own = in_order(
        core == 0, cut(branch, core * rows, rows, 0), branch_other, 1
    )
    outputs = (xfull + product(branch_own, point_weight)).astype(bf16)

    act_grad, act_grad_other = call(
        functools.partial(backward_kernel, places),
        [((rows, channels), f32)] * 2,
        [*pieces, grad_low, after(pre_grad, tap_terms[0]), grad_high],
        [pl.ANY] * (count + 3),
        [
            pltpu.VMEM((4 * rows, half), bf16),
            pltpu.VMEM((3, channels, half), bf16),
            pltpu.SemaphoreType.DMA((count + 3,)),
        ],
        6 * span * channels * half,
        24,
    )
    point_sum = added([after(term, act_grad_other) for term in point_parts])
    point_sum = cut(point_sum, y * block, block, 0) + to_y(
        cut(point_sum, (1 - y) * block, block, 0).astype(bf16)
    ).astype(f32)

    act_grad = act_grad + to_core(act_grad_other)
    scaled = act_grad * gelu_slope(normed) * norm_gain
    inner = jnp.mean(scaled * xfull, axis=-1, keepdims=True)
    input_grad = (
        cotangent.astype(f32) + ratio * scaled - xfull * ratio * ratio * ratio * inner
    ).astype(bf16)

    sums = jnp.concatenate([tap_sum, point_sum[None]], 0)
    sums = in_order(
        core == 0,
        cut(sums, core * own, own, 1),
        to_core(cut(sums, (1 - core) * own, own, 1)),
        2,
    )
    return (outputs, input_grad, sums[:3], sums[3].T)


def solution(mesh):
    placed = (
        P(("groups", "seq"), None),
        P(),
        P(None, "seq", None),
        P(),
        P(("groups", "seq"), None),
    )
    return jax.shard_map(
        local,
        mesh=mesh,
        in_specs=placed,
        out_specs=(
            P(("groups", "seq"), None),
            P(("groups", "seq"), None),
            P("groups", "seq", None),
            P("groups", "seq"),
        ),
        check_vma=False,
    )
```

```python
import functools
import math

import jax
import jax.numpy as jnp
from jax import lax
from jax.experimental import pallas as pl
from jax.experimental.pallas import tpu as pltpu
from jax.sharding import PartitionSpec as P

root_coef = math.sqrt(2.0 / math.pi)
bf16 = jnp.bfloat16
f32 = jnp.float32


def gelu_value(v):
    return 0.5 * v * (1.0 + jnp.tanh(root_coef * (v + 0.044715 * v * v * v)))


def gelu_slope(v):
    inner = jnp.tanh(root_coef * (v + 0.044715 * v * v * v))
    return 0.5 * (1.0 + inner) + 0.5 * v * (1.0 - inner * inner) * root_coef * (
        1.0 + 3.0 * 0.044715 * v * v
    )


def after(value, *others):
    return lax.optimization_barrier((value, *others))[0]


def product(left, right):
    return jnp.dot(left, right, preferred_element_type=f32)


def transposed_product(left, weight):
    return lax.dot_general(
        left, weight, (((1,), (1,)), ((), ())), preferred_element_type=f32
    )


def in_order(first, mine, other, axis):
    return jnp.where(
        first,
        jnp.concatenate([mine, other], axis),
        jnp.concatenate([other, mine], axis),
    )


MIB = 1024 * 1024


def position():
    me = lax.axis_index("seq")
    return me // 4, (me // 2) % 2, me % 2


def fetch(pairs, sems):
    copies = [
        pltpu.make_async_copy(src, dst, sems.at[i]) for i, (src, dst) in enumerate(pairs)
    ]
    for copy in copies:
        copy.start()
    for copy in copies:
        copy.wait()


def tap_copies(places, pieces, whole):
    z, y, _ = position()
    parity = lax.rem(lax.axis_index("groups"), 2)
    pairs = []
    for (shift, across, part), piece in zip(places, pieces):
        size = piece.shape[1]
        depth = lax.axis_size("seq") // 4
        source = lax.rem(z + depth - shift, depth)
        side = 1 - y if across else y
        start = source * 2 + side
        if part is not None:
            start = start * 2 + (1 - parity if part else parity)
        start = pl.multiple_of(start * size, size)
        pairs.append((piece, whole.at[:, pl.ds(start, size), :]))
    return pairs


def forward_kernel(places, *refs):
    count = len(places)
    pieces = refs[:count]
    act, act_other, edge, edge_other, slope, slope_other = refs[count : count + 6]
    branch, grad, wide, taps, sems = refs[count + 6 :]
    _, _, core = position()
    rows = act.shape[0]

    def here(start):
        return pl.ds(pl.multiple_of(start * rows, rows), rows)

    fetch(
        [
            (act, wide.at[here(1 + core)]),
            (act_other, wide.at[here(2 - core)]),
            (edge, wide.at[here(3 * core)]),
            (edge_other, wide.at[here(3 - 3 * core)]),
        ]
        + tap_copies(places, pieces, taps),
        sems,
    )
    for part, slope_in in ((core, slope), (1 - core, slope_other)):
        pre = product(wide[here(part)], taps[0])
        pre = pre + product(wide[here(part + 1)], taps[1])
        pre = pre + product(wide[here(part + 2)], taps[2])
        branch[here(part)] = gelu_value(pre).astype(bf16)
        grad[here(part)] = (slope_in[...] * gelu_slope(pre)).astype(bf16)


def targets(depth, z):
    if depth == 4:
        return [
            jnp.where(z == 0, 3, 0),
            jnp.where(z < 2, z + 2, z - 2),
            jnp.minimum(z + 1, 3),
            jnp.maximum(z - 1, 0),
            z,
        ]
    return [lax.rem(z + d, depth) for d in range(1, depth)] + [z]


def target_types(depth):
    if depth == 4:
        return [bf16, f32, bf16, bf16, f32]
    return [bf16] * (depth - 1) + [f32]


def terms_kernel(depth, act, act_other, edge, edge_other, far, far_other, mine, other, *refs):
    count = len(target_types(depth))
    outs = refs[:count]
    wide, grads, sems = refs[count:]
    z, y, core = position()
    rows = far.shape[-1]
    span = mine.shape[0]
    first = y * 2

    def at(start):
        return wide.at[:, :, pl.ds(pl.multiple_of(start * rows, rows), rows)]

    fetch(
        [
            (act.at[:, y], at(first + 1 + core)),
            (act_other.at[:, y], at(first + 2 - core)),
            (edge.at[:, y], at(first + 3 * core)),
            (edge_other.at[:, y], at(first + 3 - 3 * core)),
            (far, at((1 - y) * 4 + core)),
            (far_other, at((1 - y) * 4 + 1 - core)),
            (mine, grads.at[pl.ds(pl.multiple_of(y * span, span), span), :]),
            (other, grads.at[pl.ds(pl.multiple_of((1 - y) * span, span), span), :]),
        ],
        sems,
    )
    for out, target in zip(outs, targets(depth, z)):
        for k in range(3):
            out[k] = product(
                wide[target, :, pl.ds(k * rows, 4 * rows)], grads[...]
            ).astype(out.dtype)


def point_kernel(depth, turned, turned_other, branch, *outs):
    z, _, core = position()
    rows = turned.shape[-1]

    def here(start):
        return pl.ds(pl.multiple_of(start * rows, rows), rows)

    for out, target in zip(outs, targets(depth, z)):
        total = product(turned[target], branch[here(core)])
        total = total + product(turned_other[target], branch[here(1 - core)])
        out[...] = total.astype(out.dtype)


def backward_kernel(places, *refs):
    count = len(places)
    pieces = refs[:count]
    low, grad, high = refs[count : count + 3]
    mine, other, wide, taps, sems = refs[count + 3 :]
    _, _, core = position()
    rows = low.shape[0]
    fetch(
        [
            (low, wide.at[pl.ds(0, rows), :]),
            (grad, wide.at[pl.ds(rows, 2 * rows), :]),
            (high, wide.at[pl.ds(3 * rows, rows), :]),
        ]
        + tap_copies(places, pieces, taps),
        sems,
    )
    for out, part in ((other, 1 - core), (mine, core)):
        total = None
        for k in range(3):
            start = pl.multiple_of((part + 2 - k) * rows, rows)
            term = transposed_product(wide[pl.ds(start, rows), :], taps[k])
            total = term if total is None else total + term
        out[...] = total


def call(kernel, outs, args, specs, scratch, flops, limit):
    nbytes = sum(a.size * a.dtype.itemsize for a in args) + sum(
        math.prod(s) * jnp.dtype(t).itemsize for s, t in outs
    )
    return pl.pallas_call(
        kernel,
        out_shape=[jax.ShapeDtypeStruct(s, t) for s, t in outs],
        in_specs=[pl.BlockSpec(memory_space=m) for m in specs],
        out_specs=[pl.BlockSpec(memory_space=pltpu.VMEM)] * len(outs),
        scratch_shapes=scratch,
        compiler_params=pltpu.CompilerParams(vmem_limit_bytes=limit * MIB),
        cost_estimate=pl.CostEstimate(
            flops=flops, bytes_accessed=nbytes, transcendentals=0
        ),
    )(*args)


def local(inputs, norm_gain, dilated_weight, point_weight, cotangent):
    size = lax.axis_size("seq")
    depth = size // 4
    z, y, core = position()
    rows, channels = inputs.shape
    own = dilated_weight.shape[1]
    hidden = dilated_weight.shape[2]
    half = hidden // 2
    block = 2 * own
    span = 2 * rows

    def send(value, target):
        pairs = [(i, target(i)) for i in range(size)]
        return lax.ppermute(value, "seq", [p for p in pairs if 0 <= p[1] < size])

    def to_core(value):
        return send(value, lambda i: i ^ 1)

    def to_y(value):
        return send(value, lambda i: i ^ 2)

    def to_z(value, by):
        return send(value, lambda i: (i + 4 * by) % size)

    groups = lax.axis_size("groups")
    halved = groups % 2 == 0 and own % 16 == 0

    def to_x(value):
        return lax.ppermute(value, "groups", [(g, g ^ 1) for g in range(groups)])

    def cut(value, start, length, axis):
        return lax.dynamic_slice_in_dim(value, start, length, axis)

    def turned(value):
        return value.T.reshape(depth, 2, block, rows)

    mine = cut(dilated_weight, core * half, half, 2)
    theirs = cut(dilated_weight, (1 - core) * half, half, 2)
    inputs = after(inputs, theirs)
    cotangent = after(cotangent, theirs)
    swapped = to_core(theirs)
    if halved:
        parity = lax.axis_index("groups") % 2
        start_piece = jnp.where(core == parity, mine, swapped)
        rest_piece = jnp.where(core == parity, swapped, mine)
    else:
        start_piece = in_order(core == 0, mine, swapped, 1)
    along = [start_piece] + [to_z(start_piece, d) for d in range(1, depth)]

    xfull = inputs.astype(f32)
    ratio = lax.rsqrt(jnp.mean(xfull * xfull, axis=-1, keepdims=True) + 1e-06)
    normed = xfull * ratio * norm_gain
    act = gelu_value(normed).astype(bf16)
    edge = send(act, lambda i: i + 1 if i % 2 else i - 1)
    act_other = to_core(after(act, start_piece))
    cot_other = to_core(after(cotangent, start_piece))
    beside = [to_y(start_piece)]
    *first, edge, act_other, cot_other, act_late, cot_late = lax.optimization_barrier(
        (*along[1:], *beside, edge, act_other, cot_other, act, cotangent)
    )
    along = along[:1] + first[:-1]
    beside = first[-1:]
    point_rows = cut(point_weight, core * half, half, 0)
    branch_grad = transposed_product(cot_late, point_rows)
    branch_grad_other = transposed_product(cot_other, point_rows)
    cot_turned = turned(cot_late)
    cot_turned_other = turned(cot_other)
    act_turned = turned(act_late)
    act_turned_other = turned(act_other)
    part = 0 if halved else None
    beside += [to_y(piece) for piece in along[1:]]
    pieces = along + beside
    places = [(d, False, part) for d in range(depth)]
    places += [(d, True, part) for d in range(depth)]
    if halved:
        pieces = pieces + [rest_piece] + [to_x(c) for c in pieces[1:]]
        places = places + [(d, across, 1) for d, across, _ in places]

    edge_other = to_core(edge)
    edge_turned = turned(edge)
    far = to_y(
        cut(
            jnp.where(core == y, edge_turned, act_turned_other), 1 - y, 1, 1
        ).reshape(depth, block, rows)
    )
    edge_turned_other = turned(edge_other)

    count = len(pieces)
    branch, pre_grad = call(
        functools.partial(forward_kernel, places),
        [((span, half), bf16)] * 2,
        [
            *pieces,
            act,
            act_other,
            edge,
            after(
                edge_other,
                edge_turned_other,
                cot_turned,
                cot_turned_other,
                act_turned,
                act_turned_other,
            ),
            branch_grad,
            branch_grad_other,
        ],
        [pl.ANY] * (count + 4) + [pltpu.VMEM] * 2,
        [
            pltpu.VMEM((4 * rows, channels), bf16),
            pltpu.VMEM((3, channels, half), bf16),
            pltpu.SemaphoreType.DMA((count + 4,)),
        ],
        6 * span * channels * half,
        24,
    )

    grad_far = to_y(pre_grad)
    far_other = to_core(after(far, pre_grad))

    def line(value, pairs):
        return lax.ppermute(
            value,
            "seq",
            [(4 * a + i, 4 * b + i) for a, b in pairs for i in range(4)],
        )

    def sent(terms):
        if depth != 4:
            return [to_z(term, d + 1) for d, term in enumerate(terms[:-1])]
        three, two, up, down, _ = terms
        passing = line(three, [(0, 1), (3, 2)])
        direct = line(two.astype(bf16), [(0, 2), (3, 1)])
        up = line(up, [(0, 1), (1, 2), (2, 3)])
        down = line(down, [(1, 0), (2, 1), (3, 2)])
        joined = line((two + passing.astype(f32)).astype(bf16), [(1, 3), (2, 0)])
        return [up, down, direct, joined]

    def added(total, terms):
        for term in terms:
            total = total + term.astype(f32)
        return total

    types = target_types(depth)
    point_terms = call(
        functools.partial(point_kernel, depth),
        [((2 * block, half), t) for t in types],
        [
            cot_turned.reshape(depth, 2 * block, rows),
            cot_turned_other.reshape(depth, 2 * block, rows),
            branch,
        ],
        [pltpu.VMEM] * 3,
        [],
        2 * span * channels * half,
        16,
    )
    point_parts = sent(point_terms)

    tap_terms = call(
        functools.partial(terms_kernel, depth),
        [((3, block, half), t) for t in types],
        [
            act_turned,
            act_turned_other,
            edge_turned,
            edge_turned_other,
            far,
            far_other,
            pre_grad,
            grad_far,
        ],
        [pl.ANY] * 8,
        [
            pltpu.VMEM((depth, block, 6 * rows), bf16),
            pltpu.VMEM((2 * span, half), bf16),
            pltpu.SemaphoreType.DMA((8,)),
        ],
        6 * span * channels * half,
        24,
    )
    tap_parts = sent(tap_terms)
    first_parts = tap_parts[:-1]

    pre_grad = after(pre_grad, *first_parts)
    grad_low = send(pre_grad[rows:], lambda i: i + 2)
    grad_high = send(pre_grad[:rows], lambda i: i - 2)
    branch = after(branch, *first_parts)
    branch_other = to_core(cut(branch, (1 - core) * rows, rows, 0))
    branch_own = in_order(
        core == 0, cut(branch, core * rows, rows, 0), branch_other, 1
    )
    outputs = (xfull + product(branch_own, point_weight)).astype(bf16)
    act_grad, act_grad_other = call(
        functools.partial(backward_kernel, places),
        [((rows, channels), f32)] * 2,
        [*pieces, grad_low, pre_grad, grad_high],
        [pl.ANY] * (count + 3),
        [
            pltpu.VMEM((4 * rows, half), bf16),
            pltpu.VMEM((3, channels, half), bf16),
            pltpu.SemaphoreType.DMA((count + 3,)),
        ],
        6 * span * channels * half,
        24,
    )
    act_grad = act_grad + to_core(after(act_grad_other, tap_parts[-1]))
    scaled = act_grad * gelu_slope(normed) * norm_gain
    inner = jnp.mean(scaled * xfull, axis=-1, keepdims=True)
    input_grad = (
        cotangent.astype(f32) + ratio * scaled - xfull * ratio * ratio * ratio * inner
    ).astype(bf16)

    def halves(value, axis):
        return in_order(
            core == 0,
            cut(value, core * own, own, axis),
            to_core(cut(value, (1 - core) * own, own, axis)),
            axis + 1,
        )

    point_sum = added(
        point_terms[-1], [after(term, act_grad_other) for term in point_parts]
    )
    point_sum = cut(point_sum, y * block, block, 0) + to_y(
        cut(point_sum, (1 - y) * block, block, 0).astype(bf16)
    ).astype(f32)
    point_grad = halves(point_sum, 0).T

    tap_parts = list(
        lax.optimization_barrier((*tap_parts, outputs, input_grad, point_grad))
    )
    tap_sum = added(tap_terms[-1], tap_parts[:-3])
    return (*tap_parts[-3:-1], halves(tap_sum, 1), tap_parts[-1])


def solution(mesh):
    placed = (
        P(("groups", "seq"), None),
        P(),
        P(None, "seq", None),
        P(),
        P(("groups", "seq"), None),
    )
    return jax.shard_map(
        local,
        mesh=mesh,
        in_specs=placed,
        out_specs=(
            P(("groups", "seq"), None),
            P(("groups", "seq"), None),
            P("groups", "seq", None),
            P("groups", "seq"),
        ),
        check_vma=False,
    )
```

```python
import functools
import math

import jax
import jax.numpy as jnp
from jax import lax
from jax.experimental import pallas as pl
from jax.experimental.pallas import tpu as pltpu
from jax.sharding import PartitionSpec as P

root_coef = math.sqrt(2.0 / math.pi)
bf16 = jnp.bfloat16
f32 = jnp.float32
MIB = 1024 * 1024


def gelu_value(v):
    return 0.5 * v * (1.0 + jnp.tanh(root_coef * (v + 0.044715 * v * v * v)))


def gelu_slope(v):
    inner = jnp.tanh(root_coef * (v + 0.044715 * v * v * v))
    return 0.5 * (1.0 + inner) + 0.5 * v * (1.0 - inner * inner) * root_coef * (
        1.0 + 3.0 * 0.044715 * v * v
    )


def after(value, *others):
    return lax.optimization_barrier((value, *others))[0]


def product(left, right):
    return jnp.dot(left, right, preferred_element_type=f32)


def transposed_product(left, weight):
    return lax.dot_general(
        left, weight, (((1,), (1,)), ((), ())), preferred_element_type=f32
    )


def position():
    me = lax.axis_index("seq")
    return me // 4, lax.rem(me, 4)


def toggled(q, bit):
    low = lax.rem(q, 2)
    if bit == 0:
        return q
    if bit == 1:
        return q + 1 - 2 * low
    if bit == 2:
        return lax.rem(q + 2, 4)
    return 3 - q


def within(start, length):
    return pl.ds(pl.multiple_of(start * length, length), length)


def started(pairs, sems, first=0):
    copies = [
        pltpu.make_async_copy(src, dst, sems.at[first + i])
        for i, (src, dst) in enumerate(pairs)
    ]
    for copy in copies:
        copy.start()
    return copies


def finish(copies):
    for copy in copies:
        copy.wait()


def tap_pairs(pieces, packed):
    z, _ = position()
    depth = len(pieces)
    return [
        (piece, packed.at[:, lax.rem(z + depth - d, depth)])
        for d, piece in enumerate(pieces)
    ]


def unpack(packed, taps):
    _, depth, _, own, width = packed.shape
    quarter = width // 2
    for k in range(3):
        for i in range(2 * depth):
            for core in range(2):
                taps[k, pl.ds((2 * i + core) * own, own), :] = packed[
                    k, i // 2, i % 2, :, core * quarter : (core + 1) * quarter
                ]


def weight_kernel(depth, *refs):
    pieces = refs[:depth]
    acts = refs[depth : depth + 4]
    edge, edge_other = refs[depth + 4 : depth + 6]
    cots = refs[depth + 6 : depth + 10]
    point = refs[depth + 10]
    branch, grad = refs[depth + 11 : depth + 13]
    outs = refs[depth + 13 : -7]
    wide, wide_cot, packed, taps, grads, branches, sems = refs[-7:]
    z, q = position()
    rows = acts[0].shape[0]
    core = lax.rem(q, 2)
    first = started(
        [(act, wide.at[within(1 + toggled(q, m), rows)]) for m, act in enumerate(acts)]
        + [
            (edge, wide.at[within(5 * (1 - core), rows)]),
            (edge_other, wide.at[within(5 * core, rows)]),
        ]
        + tap_pairs(pieces, packed),
        sems,
    )
    second = started(
        [(cot, wide_cot.at[within(toggled(q, m), rows)]) for m, cot in enumerate(cots)],
        sems,
        len(first),
    )
    finish(first)
    unpack(packed, taps)
    finish(second)
    for part in range(4):
        here = pl.ds(part * rows, rows)
        slope = transposed_product(wide_cot[here], point[...])
        pre = product(wide[here], taps[0])
        pre = pre + product(wide[pl.ds((part + 1) * rows, rows)], taps[1])
        pre = pre + product(wide[pl.ds((part + 2) * rows, rows)], taps[2])
        value = gelu_value(pre)
        branch[here] = value.astype(bf16)
        branches[:, here] = value.T.astype(bf16)
        value = slope * gelu_slope(pre)
        grad[here] = value.astype(bf16)
        grads[:, here] = value.T.astype(bf16)
    width = wide.shape[1] // depth
    for i in range(depth):
        if len(outs) > 1:
            target = lax.rem(z + i + 1, depth)
            lanes = within(target, width)
            out = outs[(i + 1) % depth]
        else:
            lanes = pl.ds(i * width, width)
            out = outs[0].at[lax.rem(i + depth - z, depth)]
        for k in range(3):
            out[k] = product(
                grads[...], wide[pl.ds(k * rows, 4 * rows), lanes]
            ).astype(out.dtype)
        out[3] = product(branches[...], wide_cot[:, lanes]).astype(out.dtype)


def backward_kernel(depth, *refs):
    pieces = refs[:depth]
    low, grad, high = refs[depth : depth + 3]
    outs = refs[depth + 3 : depth + 7]
    wide, packed, taps, sems = refs[depth + 7 :]
    _, q = position()
    rows = low.shape[0]
    finish(
        started(
            [
                (low, wide.at[pl.ds(0, rows)]),
                (grad, wide.at[pl.ds(rows, 4 * rows)]),
                (high, wide.at[pl.ds(5 * rows, rows)]),
            ]
            + tap_pairs(pieces, packed),
            sems,
        )
    )
    unpack(packed, taps)
    for m in (1, 3, 2, 0):
        part = toggled(q, m)
        total = None
        for k in range(3):
            term = transposed_product(wide[within(part + 2 - k, rows)], taps[k])
            total = term if total is None else total + term
        outs[m][...] = total.astype(outs[m].dtype)


def final_kernel(*refs):
    parts = refs[:4]
    dilated, point, held = refs[4:]
    _, q = position()
    quarter = parts[0].shape[1]
    for m in range(4):
        held[m] = parts[m][...].astype(f32)
    for j in range(4):
        m = lax.rem(q + j, 2) + 2 * lax.rem(q // 2 + j // 2, 2)
        here = pl.ds(j * quarter, quarter)
        for k in range(3):
            dilated[k, :, here] = held[m, k].T
        point[here, :] = held[m, 3]


def call(kernel, outs, args, specs, scratch, flops, limit):
    nbytes = sum(a.size * a.dtype.itemsize for a in args) + sum(
        math.prod(s) * jnp.dtype(t).itemsize for s, t in outs
    )
    return pl.pallas_call(
        kernel,
        out_shape=[jax.ShapeDtypeStruct(s, t) for s, t in outs],
        in_specs=[pl.BlockSpec(memory_space=m) for m in specs],
        out_specs=[pl.BlockSpec(memory_space=pltpu.VMEM)] * len(outs),
        scratch_shapes=scratch,
        compiler_params=pltpu.CompilerParams(vmem_limit_bytes=limit * MIB),
        cost_estimate=pl.CostEstimate(
            flops=flops, bytes_accessed=nbytes, transcendentals=0
        ),
    )(*args)


def local(inputs, norm_gain, dilated_weight, point_weight, cotangent):
    size = lax.axis_size("seq")
    depth = size // 4
    z, q = position()
    core = q % 2
    y = q // 2
    rows, channels = inputs.shape
    own = dilated_weight.shape[1]
    hidden = dilated_weight.shape[2]
    quarter = hidden // 4
    flops = 8 * rows * channels * quarter

    def send(value, target):
        pairs = [(i, target(i)) for i in range(size)]
        return lax.ppermute(
            value, "seq", [p for p in pairs if p[1] is not None and 0 <= p[1] < size]
        )

    def cross(value, m):
        return send(value, lambda i: i ^ m)

    def to_z(value, by):
        return send(value, lambda i: (i + 4 * by) % size)

    def cut(value, start, length, axis):
        return lax.dynamic_slice_in_dim(value, start, length, axis)

    def in_order(first, mine, other, axis):
        return jnp.where(
            first,
            jnp.concatenate([mine, other], axis),
            jnp.concatenate([other, mine], axis),
        )

    quarters = [
        cut(dilated_weight, toggled(q, m) * quarter, quarter, 2) for m in range(4)
    ]
    inputs = after(inputs, *quarters[1:])
    cotangent = after(cotangent, *quarters[1:])
    got = [quarters[0]] + [cross(quarters[m], m) for m in range(1, 4)]
    same = in_order(core == 0, got[0], got[1], 2)
    other = in_order(core == 0, got[2], got[3], 2)
    start_piece = in_order(y == 0, same[:, None], other[:, None], 1)
    pieces = [start_piece] + [to_z(start_piece, d) for d in range(1, depth)]

    xfull = inputs.astype(f32)
    ratio = lax.rsqrt(jnp.mean(xfull * xfull, axis=-1, keepdims=True) + 1e-06)
    normed = xfull * ratio * norm_gain
    act = gelu_value(normed).astype(bf16)
    edge = send(
        act, lambda i: i + 4 if i % 4 == 3 else i - 4 if i % 4 == 0 else None
    )
    edge_across = send(
        edge, lambda i: i - 2 if i % 4 == 3 else i + 2 if i % 4 == 0 else None
    )
    edge = jnp.where(core == y, edge, edge_across)
    edge_other = cross(edge, 1)

    def around(value):
        across = cross(value, 2)
        return [value, cross(value, 1), across, cross(across, 1)]

    acts = around(act)
    cots = around(cotangent)
    point_rows = cut(point_weight, q * quarter, quarter, 0)

    width = channels // depth
    apart = width % 128 == 0
    outs = [((4, quarter, width), bf16 if d else f32) for d in range(depth)]
    if not apart:
        outs = [((depth, 4, quarter, width), f32)]
    branch, pre_grad, *terms = call(
        functools.partial(weight_kernel, depth),
        [((4 * rows, quarter), bf16)] * 2 + outs,
        [*pieces, *acts, edge, edge_other, *cots, point_rows],
        [pl.ANY] * (depth + 10) + [pltpu.VMEM],
        [
            pltpu.VMEM((6 * rows, channels), bf16),
            pltpu.VMEM((4 * rows, channels), bf16),
            pltpu.VMEM((3, depth, 2, own, 2 * quarter), bf16),
            pltpu.VMEM((3, channels, quarter), bf16),
            pltpu.VMEM((quarter, 4 * rows), bf16),
            pltpu.VMEM((quarter, 4 * rows), bf16),
            pltpu.SemaphoreType.DMA((depth + 10,)),
        ],
        8 * flops,
        40,
    )
    if not apart:
        terms = [terms[0][0]] + [terms[0][d].astype(bf16) for d in range(1, depth)]
    parts = [to_z(terms[d], d) for d in range(1, depth)]

    grad_low = send(pre_grad[3 * rows :], lambda i: i + 4)
    grad_high = send(pre_grad[:rows], lambda i: i - 4)
    shares = call(
        functools.partial(backward_kernel, depth),
        [((rows, channels), t) for t in (f32, bf16, f32, bf16)],
        [*pieces, grad_low, pre_grad, grad_high],
        [pl.ANY] * (depth + 3),
        [
            pltpu.VMEM((6 * rows, quarter), bf16),
            pltpu.VMEM((3, depth, 2, own, 2 * quarter), bf16),
            pltpu.VMEM((3, channels, quarter), bf16),
            pltpu.SemaphoreType.DMA((depth + 3,)),
        ],
        3 * flops,
        40,
    )
    mine = shares[0] + cross(shares[1], 1).astype(f32)
    far = shares[2] + cross(shares[3], 1).astype(f32)
    act_grad = mine + cross(far.astype(bf16), 2).astype(f32)
    scaled = act_grad * gelu_slope(normed) * norm_gain
    inner = jnp.mean(scaled * xfull, axis=-1, keepdims=True)
    input_grad = (
        cotangent.astype(f32) + ratio * scaled - xfull * ratio * ratio * ratio * inner
    ).astype(bf16)

    branch = branch.reshape(2, 2, rows, quarter)
    keep = cut(branch, core, 1, 1)[:, 0]
    chip = in_order(core == 0, keep, cross(cut(branch, 1 - core, 1, 1)[:, 0], 1), 2)
    keep = cut(chip, y, 1, 0)[0]
    full = in_order(y == 0, keep, cross(cut(chip, 1 - y, 1, 0)[0], 2), 1)
    outputs = (xfull + product(full, point_weight)).astype(bf16)

    total = terms[0]
    for part in parts:
        total = total + part.astype(f32)
    slices = [cut(total, toggled(q, m) * own, own, 2) for m in range(4)]
    slices = slices[:1] + [cross(slices[m].astype(bf16), m) for m in range(1, 4)]
    dilated_grad, point_grad = call(
        final_kernel,
        [((3, own, hidden), f32), ((hidden, own), f32)],
        slices,
        [pltpu.VMEM] * 4,
        [pltpu.VMEM((4, 4, quarter, own), f32)],
        1024,
        16,
    )
    return (outputs, input_grad, dilated_grad, point_grad)


def solution(mesh):
    placed = (
        P(("groups", "seq"), None),
        P(),
        P(None, "seq", None),
        P(),
        P(("groups", "seq"), None),
    )
    return jax.shard_map(
        local,
        mesh=mesh,
        in_specs=placed,
        out_specs=(
            P(("groups", "seq"), None),
            P(("groups", "seq"), None),
            P("groups", "seq", None),
            P("groups", "seq"),
        ),
        check_vma=False,
    )
```

```python
import functools
import math

import jax
import jax.numpy as jnp
from jax import lax
from jax.experimental import pallas as pl
from jax.experimental.pallas import tpu as pltpu
from jax.sharding import PartitionSpec as P

root_coef = math.sqrt(2.0 / math.pi)
bf16 = jnp.bfloat16
f32 = jnp.float32
MIB = 1024 * 1024


def gelu_value(v):
    return 0.5 * v * (1.0 + jnp.tanh(root_coef * (v + 0.044715 * v * v * v)))


def gelu_slope(v):
    inner = jnp.tanh(root_coef * (v + 0.044715 * v * v * v))
    return 0.5 * (1.0 + inner) + 0.5 * v * (1.0 - inner * inner) * root_coef * (
        1.0 + 3.0 * 0.044715 * v * v
    )


def after(value, *others):
    return lax.optimization_barrier((value, *others))[0]


def product(left, right):
    return jnp.dot(left, right, preferred_element_type=f32)


def transposed_product(left, weight):
    return lax.dot_general(
        left, weight, (((1,), (1,)), ((), ())), preferred_element_type=f32
    )


def position():
    me = lax.axis_index("seq")
    return me // 4, lax.rem(me, 4)


def toggled(q, bit):
    low = lax.rem(q, 2)
    if bit == 0:
        return q
    if bit == 1:
        return q + 1 - 2 * low
    if bit == 2:
        return lax.rem(q + 2, 4)
    return 3 - q


def within(start, length):
    return pl.ds(pl.multiple_of(start * length, length), length)


def started(pairs, sems, first=0):
    copies = []
    for i, (src, dst) in enumerate(pairs):
        sem = sems.at[first + i]
        if isinstance(src, tuple):
            chosen, src, other = src

            @pl.when(chosen)
            def _(src=src, dst=dst, sem=sem):
                pltpu.make_async_copy(src, dst, sem).start()

            @pl.when(jnp.logical_not(chosen))
            def _(src=other, dst=dst, sem=sem):
                pltpu.make_async_copy(src, dst, sem).start()

        else:
            pltpu.make_async_copy(src, dst, sem).start()
        copies.append(pltpu.make_async_copy(src, dst, sem))
    return copies


def finish(copies):
    for copy in copies:
        copy.wait()


def tap_pairs(depth, pieces, packed):
    z, _ = position()
    if depth == 4:
        own, two, up, down, passed = pieces
        return [
            (own, packed.at[:, z]),
            (two, packed.at[:, lax.rem(z + 2, 4)]),
            ((z == 0, passed, up), packed.at[:, lax.rem(z + 3, 4)]),
            ((z == 3, passed, down), packed.at[:, lax.rem(z + 1, 4)]),
        ]
    return [
        (piece, packed.at[:, lax.rem(z + depth - d, depth)])
        for d, piece in enumerate(pieces)
    ]


def targets(depth, z):
    if depth == 4:
        return [
            jnp.where(z == 0, 3, 0),
            jnp.where(z < 2, z + 2, z - 2),
            jnp.minimum(z + 1, 3),
            jnp.maximum(z - 1, 0),
            z,
        ]
    return [lax.rem(z + d, depth) for d in range(1, depth)] + [z]


def target_types(depth):
    if depth == 4:
        return [bf16, f32, bf16, bf16, f32]
    return [bf16] * (depth - 1) + [f32]


def unpack(packed, taps):
    _, depth, _, own, width = packed.shape
    quarter = width // 2
    for k in range(3):
        for i in range(2 * depth):
            for core in range(2):
                taps[k, pl.ds((2 * i + core) * own, own), :] = packed[
                    k, i // 2, i % 2, :, core * quarter : (core + 1) * quarter
                ]


def weight_kernel(depth, *refs):
    count = depth + (depth == 4)
    pieces = refs[:count]
    acts = refs[count : count + 4]
    edge, edge_other = refs[count + 4 : count + 6]
    cots = refs[count + 6 : count + 10]
    point = refs[count + 10]
    branch, grad = refs[count + 11 : count + 13]
    outs = refs[count + 13 : -7]
    wide, wide_cot, packed, taps, grads, branches, sems = refs[-7:]
    z, q = position()
    rows = acts[0].shape[0]
    core = lax.rem(q, 2)
    first = started(
        [(act, wide.at[within(1 + toggled(q, m), rows)]) for m, act in enumerate(acts)]
        + [
            (edge, wide.at[within(5 * (1 - core), rows)]),
            (edge_other, wide.at[within(5 * core, rows)]),
        ]
        + tap_pairs(depth, pieces, packed),
        sems,
    )
    second = started(
        [(cot, wide_cot.at[within(toggled(q, m), rows)]) for m, cot in enumerate(cots)],
        sems,
        len(first),
    )
    finish(first)
    unpack(packed, taps)
    finish(second)
    for part in range(4):
        here = pl.ds(part * rows, rows)
        slope = transposed_product(wide_cot[here], point[...])
        pre = product(wide[here], taps[0])
        pre = pre + product(wide[pl.ds((part + 1) * rows, rows)], taps[1])
        pre = pre + product(wide[pl.ds((part + 2) * rows, rows)], taps[2])
        value = gelu_value(pre)
        branch[here] = value.astype(bf16)
        branches[:, here] = value.T.astype(bf16)
        value = slope * gelu_slope(pre)
        grad[here] = value.astype(bf16)
        grads[:, here] = value.T.astype(bf16)
    width = wide.shape[1] // depth
    if len(outs) > 1:
        where = [within(target, width) for target in targets(depth, z)]
    else:
        where = [pl.ds(i * width, width) for i in range(depth)]
    for i, lanes in enumerate(where):
        if len(outs) > 1:
            out = outs[i]
        else:
            out = outs[0].at[lax.rem(i + depth - z, depth)]
        for k in range(3):
            out[k] = product(
                grads[...], wide[pl.ds(k * rows, 4 * rows), lanes]
            ).astype(out.dtype)
        out[3] = product(branches[...], wide_cot[:, lanes]).astype(out.dtype)


def backward_kernel(depth, *refs):
    count = depth + (depth == 4)
    pieces = refs[:count]
    low, grad, high = refs[count : count + 3]
    outs = refs[count + 3 : count + 7]
    wide, packed, taps, sems = refs[count + 7 :]
    _, q = position()
    rows = low.shape[0]
    finish(
        started(
            [
                (low, wide.at[pl.ds(0, rows)]),
                (grad, wide.at[pl.ds(rows, 4 * rows)]),
                (high, wide.at[pl.ds(5 * rows, rows)]),
            ]
            + tap_pairs(depth, pieces, packed),
            sems,
        )
    )
    unpack(packed, taps)
    for m in (1, 3, 2, 0):
        part = toggled(q, m)
        total = None
        for k in range(3):
            term = transposed_product(wide[within(part + 2 - k, rows)], taps[k])
            total = term if total is None else total + term
        outs[m][...] = total.astype(outs[m].dtype)


def final_kernel(*refs):
    parts = refs[:4]
    dilated, point, held = refs[4:]
    _, q = position()
    quarter = parts[0].shape[1]
    for m in range(4):
        held[m] = parts[m][...].astype(f32)
    for j in range(4):
        m = lax.rem(q + j, 2) + 2 * lax.rem(q // 2 + j // 2, 2)
        here = pl.ds(j * quarter, quarter)
        for k in range(3):
            dilated[k, :, here] = held[m, k].T
        point[here, :] = held[m, 3]


def call(kernel, outs, args, specs, scratch, flops, limit):
    nbytes = sum(a.size * a.dtype.itemsize for a in args) + sum(
        math.prod(s) * jnp.dtype(t).itemsize for s, t in outs
    )
    return pl.pallas_call(
        kernel,
        out_shape=[jax.ShapeDtypeStruct(s, t) for s, t in outs],
        in_specs=[pl.BlockSpec(memory_space=m) for m in specs],
        out_specs=[pl.BlockSpec(memory_space=pltpu.VMEM)] * len(outs),
        scratch_shapes=scratch,
        compiler_params=pltpu.CompilerParams(vmem_limit_bytes=limit * MIB),
        cost_estimate=pl.CostEstimate(
            flops=flops, bytes_accessed=nbytes, transcendentals=0
        ),
    )(*args)


def local(inputs, norm_gain, dilated_weight, point_weight, cotangent):
    size = lax.axis_size("seq")
    depth = size // 4
    z, q = position()
    core = q % 2
    y = q // 2
    rows, channels = inputs.shape
    own = dilated_weight.shape[1]
    hidden = dilated_weight.shape[2]
    quarter = hidden // 4
    flops = 8 * rows * channels * quarter

    def send(value, target):
        pairs = [(i, target(i)) for i in range(size)]
        return lax.ppermute(
            value, "seq", [p for p in pairs if p[1] is not None and 0 <= p[1] < size]
        )

    def cross(value, m):
        return send(value, lambda i: i ^ m)

    def to_z(value, by):
        return send(value, lambda i: (i + 4 * by) % size)

    def cut(value, start, length, axis):
        return lax.dynamic_slice_in_dim(value, start, length, axis)

    def in_order(first, mine, other, axis):
        return jnp.where(
            first,
            jnp.concatenate([mine, other], axis),
            jnp.concatenate([other, mine], axis),
        )

    quarters = [
        cut(dilated_weight, toggled(q, m) * quarter, quarter, 2) for m in range(4)
    ]
    inputs = after(inputs, *quarters[1:])
    cotangent = after(cotangent, *quarters[1:])
    got = [quarters[0]] + [cross(quarters[m], m) for m in range(1, 4)]
    same = in_order(core == 0, got[0], got[1], 2)
    other = in_order(core == 0, got[2], got[3], 2)
    start_piece = in_order(y == 0, same[:, None], other[:, None], 1)

    def line(value, pairs):
        return lax.ppermute(
            value,
            "seq",
            [(4 * a + i, 4 * b + i) for a, b in pairs for i in range(4)],
        )

    if depth == 4:
        two = to_z(start_piece, 2)
        up = line(start_piece, [(0, 1), (1, 2), (2, 3)])
        down = line(start_piece, [(1, 0), (2, 1), (3, 2)])
        pieces = [start_piece, two, up, down, line(two, [(2, 3), (1, 0)])]
    else:
        pieces = [start_piece] + [to_z(start_piece, d) for d in range(1, depth)]

    xfull = inputs.astype(f32)
    ratio = lax.rsqrt(jnp.mean(xfull * xfull, axis=-1, keepdims=True) + 1e-06)
    normed = xfull * ratio * norm_gain
    act = gelu_value(normed).astype(bf16)
    act_late = after(act, start_piece)
    cot_late = after(cotangent, start_piece)
    act_across = cross(act_late, 2)
    edge = send(
        jnp.where(core == y, act_late, act_across),
        lambda i: i + 4 if i % 2 else i - 4,
    )
    edge_other = cross(edge, 1)
    cot_across = cross(after(cot_late, act_across), 2)
    acts = [act_late, cross(act_late, 1), act_across, cross(act_across, 1)]
    cots = [cot_late, cross(cot_late, 1), cot_across, cross(cot_across, 1)]
    point_rows = cut(point_weight, q * quarter, quarter, 0)

    width = channels // depth
    apart = width % 128 == 0
    outs = [((4, quarter, width), t) for t in target_types(depth)]
    if not apart:
        outs = [((depth, 4, quarter, width), f32)]
    branch, pre_grad, *terms = call(
        functools.partial(weight_kernel, depth),
        [((4 * rows, quarter), bf16)] * 2 + outs,
        [*pieces, *acts, edge, edge_other, *cots, point_rows],
        [pl.ANY] * (len(pieces) + 10) + [pltpu.VMEM],
        [
            pltpu.VMEM((6 * rows, channels), bf16),
            pltpu.VMEM((4 * rows, channels), bf16),
            pltpu.VMEM((3, depth, 2, own, 2 * quarter), bf16),
            pltpu.VMEM((3, channels, quarter), bf16),
            pltpu.VMEM((quarter, 4 * rows), bf16),
            pltpu.VMEM((quarter, 4 * rows), bf16),
            pltpu.SemaphoreType.DMA((depth + 10,)),
        ],
        8 * flops,
        40,
    )
    if not apart:
        terms = [terms[0][d].astype(bf16) for d in range(1, depth)] + [terms[0][0]]
    if depth == 4:
        three, two, up, down, total = terms
        passed = line(three, [(0, 1), (3, 2)])
        joined = line((two + passed.astype(f32)).astype(bf16), [(1, 3), (2, 0)])
        parts = [
            line(two.astype(bf16), [(0, 2), (3, 1)]),
            line(up, [(0, 1), (1, 2), (2, 3)]),
            line(down, [(1, 0), (2, 1), (3, 2)]),
            joined,
        ]
    else:
        total = terms[-1]
        parts = [to_z(term, d + 1) for d, term in enumerate(terms[:-1])]

    grad_low = send(pre_grad[3 * rows :], lambda i: i + 4)
    grad_high = send(pre_grad[:rows], lambda i: i - 4)
    shares = call(
        functools.partial(backward_kernel, depth),
        [((rows, channels), t) for t in (f32, bf16, f32, bf16)],
        [*pieces, grad_low, pre_grad, grad_high],
        [pl.ANY] * (len(pieces) + 3),
        [
            pltpu.VMEM((6 * rows, quarter), bf16),
            pltpu.VMEM((3, depth, 2, own, 2 * quarter), bf16),
            pltpu.VMEM((3, channels, quarter), bf16),
            pltpu.SemaphoreType.DMA((depth + 3,)),
        ],
        3 * flops,
        40,
    )
    mine = shares[0] + cross(shares[1], 1).astype(f32)
    far = shares[2] + cross(shares[3], 1).astype(f32)
    act_grad = mine + cross(far.astype(bf16), 2).astype(f32)
    scaled = act_grad * gelu_slope(normed) * norm_gain
    inner = jnp.mean(scaled * xfull, axis=-1, keepdims=True)
    input_grad = (
        cotangent.astype(f32) + ratio * scaled - xfull * ratio * ratio * ratio * inner
    ).astype(bf16)

    branch = branch.reshape(2, 2, rows, quarter)
    keep = cut(branch, core, 1, 1)[:, 0]
    chip = in_order(core == 0, keep, cross(cut(branch, 1 - core, 1, 1)[:, 0], 1), 2)
    keep = cut(chip, y, 1, 0)[0]
    full = in_order(y == 0, keep, cross(cut(chip, 1 - y, 1, 0)[0], 2), 1)
    outputs = (xfull + product(full, point_weight)).astype(bf16)

    for part in parts:
        total = total + part.astype(f32)
    slices = [cut(total, toggled(q, m) * own, own, 2) for m in range(4)]
    slices = slices[:1] + [cross(slices[m].astype(bf16), m) for m in range(1, 4)]
    slices[3] = after(slices[3], input_grad, outputs)
    dilated_grad, point_grad = call(
        final_kernel,
        [((3, own, hidden), f32), ((hidden, own), f32)],
        slices,
        [pltpu.VMEM] * 4,
        [pltpu.VMEM((4, 4, quarter, own), f32)],
        1024,
        16,
    )
    return (outputs, input_grad, dilated_grad, point_grad)


def solution(mesh):
    placed = (
        P(("groups", "seq"), None),
        P(),
        P(None, "seq", None),
        P(),
        P(("groups", "seq"), None),
    )
    return jax.shard_map(
        local,
        mesh=mesh,
        in_specs=placed,
        out_specs=(
            P(("groups", "seq"), None),
            P(("groups", "seq"), None),
            P("groups", "seq", None),
            P("groups", "seq"),
        ),
        check_vma=False,
    )
```

```python
import functools
import math

import jax
import jax.numpy as jnp
from jax import lax
from jax.experimental import pallas as pl
from jax.experimental.pallas import tpu as pltpu
from jax.sharding import PartitionSpec as P

root_coef = math.sqrt(2.0 / math.pi)
bf16 = jnp.bfloat16
f32 = jnp.float32
MIB = 1024 * 1024


def gelu_value(v):
    return 0.5 * v * (1.0 + jnp.tanh(root_coef * (v + 0.044715 * v * v * v)))


def gelu_slope(v):
    inner = jnp.tanh(root_coef * (v + 0.044715 * v * v * v))
    return 0.5 * (1.0 + inner) + 0.5 * v * (1.0 - inner * inner) * root_coef * (
        1.0 + 3.0 * 0.044715 * v * v
    )


def after(value, *others):
    return lax.optimization_barrier((value, *others))[0]


def product(left, right):
    return jnp.dot(left, right, preferred_element_type=f32)


def transposed_product(left, weight):
    return lax.dot_general(
        left, weight, (((1,), (1,)), ((), ())), preferred_element_type=f32
    )


def position():
    me = lax.axis_index("seq")
    return me // 4, lax.rem(me, 4)


def toggled(q, bit):
    low = lax.rem(q, 2)
    if bit == 0:
        return q
    if bit == 1:
        return q + 1 - 2 * low
    if bit == 2:
        return lax.rem(q + 2, 4)
    return 3 - q


def within(start, length):
    return pl.ds(pl.multiple_of(start * length, length), length)


def started(pairs, sems, first=0):
    copies = []
    for i, (src, dst) in enumerate(pairs):
        sem = sems.at[first + i]
        if isinstance(src, tuple):
            chosen, src, other = src

            @pl.when(chosen)
            def _(src=src, dst=dst, sem=sem):
                pltpu.make_async_copy(src, dst, sem).start()

            @pl.when(jnp.logical_not(chosen))
            def _(src=other, dst=dst, sem=sem):
                pltpu.make_async_copy(src, dst, sem).start()

        else:
            pltpu.make_async_copy(src, dst, sem).start()
        copies.append(pltpu.make_async_copy(src, dst, sem))
    return copies


def finish(copies):
    for copy in copies:
        copy.wait()


def tap_pairs(depth, pieces, packed):
    z, _ = position()
    if depth == 4:
        own, *ups = pieces[:4]
        downs = pieces[4:]
        return [(own, packed.at[:, z])] + [
            ((z > j, ups[j], downs[2 - j]), packed.at[:, lax.rem(z + 3 - j, 4)])
            for j in range(3)
        ]
    return [
        (piece, packed.at[:, lax.rem(z + depth - d, depth)])
        for d, piece in enumerate(pieces)
    ]


def targets(depth, z):
    if depth == 4:
        return [
            jnp.where(z == 0, 3, 0),
            jnp.where(z < 2, z + 2, z - 2),
            jnp.minimum(z + 1, 3),
            jnp.maximum(z - 1, 0),
            z,
        ]
    return [lax.rem(z + d, depth) for d in range(1, depth)] + [z]


def target_types(depth):
    if depth == 4:
        return [bf16, f32, f32, f32, f32]
    return [bf16] * (depth - 1) + [f32]


def unpack(packed, taps):
    _, depth, _, own, width = packed.shape
    quarter = width // 2
    for k in range(3):
        for i in range(2 * depth):
            for core in range(2):
                taps[k, pl.ds((2 * i + core) * own, own), :] = packed[
                    k, i // 2, i % 2, :, core * quarter : (core + 1) * quarter
                ]


def weight_kernel(depth, *refs):
    count = depth + 3 * (depth == 4)
    pieces = refs[:count]
    acts = refs[count : count + 4]
    edge, edge_other = refs[count + 4 : count + 6]
    cots = refs[count + 6 : count + 10]
    point = refs[count + 10]
    refs = refs[count + 11 :]
    results = (len(refs) - 7) // 2
    stores, (wide, wide_cot, packed, taps, grads, branches, sems) = (
        refs[:results],
        refs[results : results + 7],
    )
    branch, grad, *outs = refs[results + 7 :]
    z, q = position()
    rows = acts[0].shape[0]
    core = lax.rem(q, 2)
    first = started(
        [(act, wide.at[within(1 + toggled(q, m), rows)]) for m, act in enumerate(acts)]
        + [
            (edge, wide.at[within(5 * (1 - core), rows)]),
            (edge_other, wide.at[within(5 * core, rows)]),
        ]
        + tap_pairs(depth, pieces, packed),
        sems,
    )
    second = started(
        [(cot, wide_cot.at[within(toggled(q, m), rows)]) for m, cot in enumerate(cots)],
        sems,
        len(first),
    )
    base = len(first) + len(second)
    finish(first)
    unpack(packed, taps)
    finish(second)
    for part in range(4):
        here = pl.ds(part * rows, rows)
        slope = transposed_product(wide_cot[here], point[...])
        pre = product(wide[here], taps[0])
        pre = pre + product(wide[pl.ds((part + 1) * rows, rows)], taps[1])
        pre = pre + product(wide[pl.ds((part + 2) * rows, rows)], taps[2])
        value = gelu_value(pre)
        branch[here] = value.astype(bf16)
        branches[:, here] = value.T.astype(bf16)
        value = slope * gelu_slope(pre)
        grad[here] = value.astype(bf16)
        grads[:, here] = value.T.astype(bf16)
    last = started([(grad, stores[1]), (branch, stores[0])], sems, base)
    width = wide.shape[1] // depth
    if len(outs) > 1:
        where = [within(target, width) for target in targets(depth, z)]
    else:
        where = [pl.ds(i * width, width) for i in range(depth)]
    for i, lanes in enumerate(where):
        if len(outs) > 1:
            out = outs[i]
        else:
            out = outs[0].at[lax.rem(i + depth - z, depth)]
        for k in range(3):
            out[k] = product(
                grads[...], wide[pl.ds(k * rows, 4 * rows), lanes]
            ).astype(out.dtype)
        out[3] = product(branches[...], wide_cot[:, lanes]).astype(out.dtype)
        if len(outs) > 1:
            last += started([(out, stores[2 + i])], sems, base + 2 + i)
    if len(outs) == 1:
        last += started([(outs[0], stores[2])], sems, base + 2)
    finish(last)


def backward_kernel(depth, *refs):
    count = depth + 3 * (depth == 4)
    pieces = refs[:count]
    low, grad, high = refs[count : count + 3]
    stores = refs[count + 3 : count + 7]
    wide, packed, taps, sems = refs[count + 7 : count + 11]
    outs = refs[count + 11 :]
    _, q = position()
    rows = low.shape[0]
    finish(
        started(
            [
                (low, wide.at[pl.ds(0, rows)]),
                (grad, wide.at[pl.ds(rows, 4 * rows)]),
                (high, wide.at[pl.ds(5 * rows, rows)]),
            ]
            + tap_pairs(depth, pieces, packed),
            sems,
        )
    )
    unpack(packed, taps)
    last = []
    for m in (1, 3, 2, 0):
        part = toggled(q, m)
        total = None
        for k in range(3):
            term = transposed_product(wide[within(part + 2 - k, rows)], taps[k])
            total = term if total is None else total + term
        outs[m][...] = total.astype(outs[m].dtype)
        last += started([(outs[m], stores[m])], sems, count + 3 + m)
    finish(last)


def final_kernel(*refs):
    parts = refs[:4]
    dilated, point, held = refs[4:]
    _, q = position()
    quarter = parts[0].shape[1]
    for m in range(4):
        held[m] = parts[m][...].astype(f32)
    for j in range(4):
        m = lax.rem(q + j, 2) + 2 * lax.rem(q // 2 + j // 2, 2)
        here = pl.ds(j * quarter, quarter)
        for k in range(3):
            dilated[k, :, here] = held[m, k].T
        point[here, :] = held[m, 3]


def call(kernel, outs, args, specs, scratch, flops, limit, kept=pltpu.VMEM):
    nbytes = sum(a.size * a.dtype.itemsize for a in args) + sum(
        math.prod(s) * jnp.dtype(t).itemsize for s, t in outs
    )
    return pl.pallas_call(
        kernel,
        out_shape=[jax.ShapeDtypeStruct(s, t) for s, t in outs],
        in_specs=[pl.BlockSpec(memory_space=m) for m in specs],
        out_specs=[pl.BlockSpec(memory_space=kept)] * len(outs),
        scratch_shapes=scratch,
        compiler_params=pltpu.CompilerParams(vmem_limit_bytes=limit * MIB),
        cost_estimate=pl.CostEstimate(
            flops=flops, bytes_accessed=nbytes, transcendentals=0
        ),
    )(*args)


def local(inputs, norm_gain, dilated_weight, point_weight, cotangent):
    size = lax.axis_size("seq")
    depth = size // 4
    z, q = position()
    core = q % 2
    y = q // 2
    rows, channels = inputs.shape
    own = dilated_weight.shape[1]
    hidden = dilated_weight.shape[2]
    quarter = hidden // 4
    flops = 8 * rows * channels * quarter

    def send(value, target):
        pairs = [(i, target(i)) for i in range(size)]
        return lax.ppermute(
            value, "seq", [p for p in pairs if p[1] is not None and 0 <= p[1] < size]
        )

    def cross(value, m):
        return send(value, lambda i: i ^ m)

    def to_z(value, by):
        return send(value, lambda i: (i + 4 * by) % size)

    def cut(value, start, length, axis):
        return lax.dynamic_slice_in_dim(value, start, length, axis)

    def in_order(first, mine, other, axis):
        return jnp.where(
            first,
            jnp.concatenate([mine, other], axis),
            jnp.concatenate([other, mine], axis),
        )

    quarters = [
        cut(dilated_weight, toggled(q, m) * quarter, quarter, 2) for m in range(4)
    ]
    inputs = after(inputs, *quarters[1:])
    cotangent = after(cotangent, *quarters[1:])
    got = [quarters[0]] + [cross(quarters[m], m) for m in range(1, 4)]
    same = in_order(core == 0, got[0], got[1], 2)
    other = in_order(core == 0, got[2], got[3], 2)
    start_piece = in_order(y == 0, same[:, None], other[:, None], 1)

    def line(value, pairs):
        return lax.ppermute(
            value,
            "seq",
            [(4 * a + i, 4 * b + i) for a, b in pairs for i in range(4)],
        )

    if depth == 4:
        ups, downs = [start_piece], [start_piece]
        for j in range(3):
            ups.append(line(ups[-1], [(a, a + 1) for a in range(j, 3)]))
            downs.append(line(downs[-1], [(a + 1, a) for a in range(3 - j)]))
        pieces = ups + downs[1:]
    else:
        pieces = [start_piece] + [to_z(start_piece, d) for d in range(1, depth)]

    xfull = inputs.astype(f32)
    ratio = lax.rsqrt(jnp.mean(xfull * xfull, axis=-1, keepdims=True) + 1e-06)
    normed = xfull * ratio * norm_gain
    act = gelu_value(normed).astype(bf16)
    act_late = after(act, start_piece)
    cot_late = after(cotangent, start_piece)
    act_across = cross(act_late, 2)
    if depth == 4:
        act_across, pieces[1], pieces[4] = lax.optimization_barrier(
            (act_across, pieces[1], pieces[4])
        )
    edge = send(
        jnp.where(core == y, act_late, act_across),
        lambda i: i + 4 if i % 2 else i - 4,
    )
    edge_other = cross(edge, 1)
    cot_across = cross(after(cot_late, act_across), 2)
    acts = [act_late, cross(act_late, 1), act_across, cross(act_across, 1)]
    cots = [cot_late, cross(cot_late, 1), cot_across, cross(cot_across, 1)]
    point_rows = cut(point_weight, q * quarter, quarter, 0)

    width = channels // depth
    apart = width % 128 == 0
    outs = [((4, quarter, width), t) for t in target_types(depth)]
    if not apart:
        outs = [((depth, 4, quarter, width), f32)]
    weight_outs = [((4 * rows, quarter), bf16)] * 2 + outs
    branch, pre_grad, *terms = call(
        functools.partial(weight_kernel, depth),
        weight_outs,
        [*pieces, *acts, edge, edge_other, *cots, point_rows],
        [pltpu.HBM] * (len(pieces) + 10) + [pltpu.VMEM],
        [
            pltpu.VMEM((6 * rows, channels), bf16),
            pltpu.VMEM((4 * rows, channels), bf16),
            pltpu.VMEM((3, depth, 2, own, 2 * quarter), bf16),
            pltpu.VMEM((3, channels, quarter), bf16),
            pltpu.VMEM((quarter, 4 * rows), bf16),
            pltpu.VMEM((quarter, 4 * rows), bf16),
            pltpu.SemaphoreType.DMA((2 * len(pieces) + 14,)),
            *[pltpu.VMEM(*out) for out in weight_outs],
        ],
        8 * flops,
        40,
        pltpu.HBM,
    )
    if not apart:
        terms = [terms[0][d].astype(bf16) for d in range(1, depth)] + [terms[0][0]]
    if depth == 4:
        three, two, up, down, total = terms
        far = line(three, [(0, 1), (3, 2)])
        joined = (two + far.astype(f32)).astype(bf16)
        near_up = line(joined, [(0, 1), (1, 2)])
        near_down = line(joined, [(3, 2), (2, 1)])
        up = (up + near_up.astype(f32)).astype(bf16)
        down = (down + near_down.astype(f32)).astype(bf16)
        parts = [
            line(up, [(0, 1), (1, 2), (2, 3)]),
            line(down, [(1, 0), (2, 1), (3, 2)]),
        ]
    else:
        total = terms[-1]
        parts = [to_z(term, d + 1) for d, term in enumerate(terms[:-1])]

    grad_low = send(pre_grad[3 * rows :], lambda i: i + 4)
    grad_high = send(pre_grad[:rows], lambda i: i - 4)
    share_outs = [((rows, channels), t) for t in (f32, bf16, f32, bf16)]
    shares = call(
        functools.partial(backward_kernel, depth),
        share_outs,
        [*pieces, grad_low, pre_grad, grad_high],
        [pltpu.HBM] * (len(pieces) + 3),
        [
            pltpu.VMEM((6 * rows, quarter), bf16),
            pltpu.VMEM((3, depth, 2, own, 2 * quarter), bf16),
            pltpu.VMEM((3, channels, quarter), bf16),
            pltpu.SemaphoreType.DMA((len(pieces) + 7,)),
            *[pltpu.VMEM(*out) for out in share_outs],
        ],
        3 * flops,
        40,
        pltpu.HBM,
    )
    mine = shares[0] + cross(shares[1], 1).astype(f32)
    far = shares[2] + cross(shares[3], 1).astype(f32)
    act_grad = mine + cross(far.astype(bf16), 2).astype(f32)
    scaled = act_grad * gelu_slope(normed) * norm_gain
    inner = jnp.mean(scaled * xfull, axis=-1, keepdims=True)
    input_grad = (
        cotangent.astype(f32) + ratio * scaled - xfull * ratio * ratio * ratio * inner
    ).astype(bf16)

    branch = branch.reshape(2, 2, rows, quarter)
    keep = cut(branch, core, 1, 1)[:, 0]
    chip = in_order(core == 0, keep, cross(cut(branch, 1 - core, 1, 1)[:, 0], 1), 2)
    keep = cut(chip, y, 1, 0)[0]
    full = in_order(y == 0, keep, cross(cut(chip, 1 - y, 1, 0)[0], 2), 1)
    outputs = (xfull + product(full, point_weight)).astype(bf16)

    for part in parts:
        total = total + part.astype(f32)
    slices = [cut(total, toggled(q, m) * own, own, 2) for m in range(4)]
    slices = slices[:1] + [cross(slices[m].astype(bf16), m) for m in range(1, 4)]
    slices[3] = after(slices[3], input_grad, outputs)
    dilated_grad, point_grad = call(
        final_kernel,
        [((3, own, hidden), f32), ((hidden, own), f32)],
        slices,
        [pltpu.VMEM] * 4,
        [pltpu.VMEM((4, 4, quarter, own), f32)],
        1024,
        16,
    )
    return (outputs, input_grad, dilated_grad, point_grad)


def solution(mesh):
    placed = (
        P(("groups", "seq"), None),
        P(),
        P(None, "seq", None),
        P(),
        P(("groups", "seq"), None),
    )
    return jax.shard_map(
        local,
        mesh=mesh,
        in_specs=placed,
        out_specs=(
            P(("groups", "seq"), None),
            P(("groups", "seq"), None),
            P("groups", "seq", None),
            P("groups", "seq"),
        ),
        check_vma=False,
    )
```

```python
import functools
import math

import jax
import jax.numpy as jnp
from jax import lax
from jax.experimental import pallas as pl
from jax.experimental.pallas import tpu as pltpu
from jax.sharding import PartitionSpec as P

root_coef = math.sqrt(2.0 / math.pi)
bf16 = jnp.bfloat16
f32 = jnp.float32
MIB = 1024 * 1024


def gelu_value(v):
    return 0.5 * v * (1.0 + jnp.tanh(root_coef * (v + 0.044715 * v * v * v)))


def gelu_slope(v):
    inner = jnp.tanh(root_coef * (v + 0.044715 * v * v * v))
    return 0.5 * (1.0 + inner) + 0.5 * v * (1.0 - inner * inner) * root_coef * (
        1.0 + 3.0 * 0.044715 * v * v
    )


def after(value, *others):
    return lax.optimization_barrier((value, *others))[0]


def product(left, right):
    return jnp.dot(left, right, preferred_element_type=f32)


def transposed_product(left, weight):
    return lax.dot_general(
        left, weight, (((1,), (1,)), ((), ())), preferred_element_type=f32
    )


def position():
    me = lax.axis_index("seq")
    return me // 4, lax.rem(me, 4)


def toggled(q, bit):
    low = lax.rem(q, 2)
    if bit == 0:
        return q
    if bit == 1:
        return q + 1 - 2 * low
    if bit == 2:
        return lax.rem(q + 2, 4)
    return 3 - q


def within(start, length):
    return pl.ds(pl.multiple_of(start * length, length), length)


def started(pairs, sems, first=0):
    copies = []
    for i, (src, dst) in enumerate(pairs):
        sem = sems.at[first + i]
        if isinstance(src, tuple):
            chosen, src, other = src

            @pl.when(chosen)
            def _(src=src, dst=dst, sem=sem):
                pltpu.make_async_copy(src, dst, sem).start()

            @pl.when(jnp.logical_not(chosen))
            def _(src=other, dst=dst, sem=sem):
                pltpu.make_async_copy(src, dst, sem).start()

        else:
            pltpu.make_async_copy(src, dst, sem).start()
        copies.append(pltpu.make_async_copy(src, dst, sem))
    return copies


def finish(copies):
    for copy in copies:
        copy.wait()


def tap_pairs(depth, pieces, packed):
    z, _ = position()
    if depth == 4:
        own, *ups = pieces[:4]
        downs = pieces[4:]
        return [(own, packed.at[:, z])] + [
            ((z > j, ups[j], downs[2 - j]), packed.at[:, lax.rem(z + 3 - j, 4)])
            for j in range(3)
        ]
    return [
        (piece, packed.at[:, lax.rem(z + depth - d, depth)])
        for d, piece in enumerate(pieces)
    ]


def roles(depth, z):
    if depth == 4:
        return [
            (3 * lax.rem(z + 1, 2), [bf16, f32]),
            (lax.rem(z + 2, 4), [f32]),
            (1 + lax.rem(z, 2), [f32]),
            (z, [f32]),
        ]
    return [(lax.rem(z + d, depth), [bf16]) for d in range(1, depth)] + [(z, [f32])]


def unpack(packed, taps):
    _, depth, _, own, width = packed.shape
    quarter = width // 2
    for k in range(3):
        for i in range(2 * depth):
            for core in range(2):
                taps[k, pl.ds((2 * i + core) * own, own), :] = packed[
                    k, i // 2, i % 2, :, core * quarter : (core + 1) * quarter
                ]


def weight_kernel(depth, *refs):
    count = depth + 3 * (depth == 4)
    pieces = refs[:count]
    acts = refs[count : count + 4]
    edge, edge_other = refs[count + 4 : count + 6]
    cots = refs[count + 6 : count + 10]
    point = refs[count + 10]
    refs = refs[count + 11 :]
    results = (len(refs) - 8) // 2
    stores, (wide, wide_cot, packed, taps, grads, branches, slopes, sems) = (
        refs[:results],
        refs[results : results + 8],
    )
    branch, grad, *outs = refs[results + 8 :]
    z, q = position()
    rows = acts[0].shape[0]
    core = lax.rem(q, 2)
    second = started(
        [(cot, wide_cot.at[within(toggled(q, m), rows)]) for m, cot in enumerate(cots)],
        sems,
    )
    first = started(
        [(act, wide.at[within(1 + toggled(q, m), rows)]) for m, act in enumerate(acts)]
        + [
            (edge, wide.at[within(5 * (1 - core), rows)]),
            (edge_other, wide.at[within(5 * core, rows)]),
        ]
        + tap_pairs(depth, pieces, packed),
        sems,
        len(second),
    )
    base = len(first) + len(second)
    finish(second)
    for part in range(4):
        here = pl.ds(part * rows, rows)
        slopes[here] = transposed_product(wide_cot[here], point[...])
    finish(first)
    unpack(packed, taps)
    for part in range(4):
        here = pl.ds(part * rows, rows)
        pre = product(wide[here], taps[0])
        pre = pre + product(wide[pl.ds((part + 1) * rows, rows)], taps[1])
        pre = pre + product(wide[pl.ds((part + 2) * rows, rows)], taps[2])
        value = gelu_value(pre)
        branch[here] = value.astype(bf16)
        branches[:, here] = value.T.astype(bf16)
        value = slopes[here] * gelu_slope(pre)
        grad[here] = value.astype(bf16)
        grads[:, here] = value.T.astype(bf16)
    last = started([(grad, stores[1]), (branch, stores[0])], sems, base)
    width = wide.shape[1] // depth
    if len(outs) == 1:
        for i in range(depth):
            lanes = pl.ds(i * width, width)
            out = outs[0].at[lax.rem(i + depth - z, depth)]
            for k in range(3):
                out[k] = product(grads[...], wide[pl.ds(k * rows, 4 * rows), lanes])
            out[3] = product(branches[...], wide_cot[:, lanes])
        last += started([(outs[0], stores[2])], sems, base + 2)
    else:
        i = 0
        for target, types in roles(depth, z):
            lanes = within(target, width)
            same = outs[i : i + len(types)]
            for k in range(4):
                if k < 3:
                    value = product(
                        grads[...], wide[pl.ds(k * rows, 4 * rows), lanes]
                    )
                else:
                    value = product(branches[...], wide_cot[:, lanes])
                for out in same:
                    out[k] = value.astype(out.dtype)
            i += len(types)
            if depth != 4:
                last += started([(same[0], stores[1 + i])], sems, base + 1 + i)
            elif i == 2:
                last += started([(outs[0], stores[2])], sems, base + 2)
            elif i == 3:
                last += started([(outs[2], stores[3])], sems, base + 3)
            elif i == 4:
                last += started(
                    [
                        ((z == 2, outs[1], outs[3]), stores[4]),
                        ((z == 1, outs[1], outs[3]), stores[5]),
                    ],
                    sems,
                    base + 4,
                )
            else:
                last += started([(outs[4], stores[6])], sems, base + 6)
    finish(last)


def backward_kernel(depth, *refs):
    count = depth + 3 * (depth == 4)
    pieces = refs[:count]
    low, grad, high = refs[count : count + 3]
    stores = refs[count + 3 : count + 7]
    wide, packed, taps, sems = refs[count + 7 : count + 11]
    outs = refs[count + 11 :]
    _, q = position()
    rows = low.shape[0]
    finish(
        started(
            [
                (low, wide.at[pl.ds(0, rows)]),
                (grad, wide.at[pl.ds(rows, 4 * rows)]),
                (high, wide.at[pl.ds(5 * rows, rows)]),
            ]
            + tap_pairs(depth, pieces, packed),
            sems,
        )
    )
    unpack(packed, taps)
    last = []
    for m in (1, 3, 2, 0):
        part = toggled(q, m)
        total = None
        for k in range(3):
            term = transposed_product(wide[within(part + 2 - k, rows)], taps[k])
            total = term if total is None else total + term
        outs[m][...] = total.astype(outs[m].dtype)
        last += started([(outs[m], stores[m])], sems, count + 3 + m)
    finish(last)


def final_kernel(*refs):
    parts = refs[:4]
    dilated, point, held = refs[4:]
    _, q = position()
    quarter = parts[0].shape[1]
    for m in range(4):
        held[m] = parts[m][...].astype(f32)
    for j in range(4):
        m = lax.rem(q + j, 2) + 2 * lax.rem(q // 2 + j // 2, 2)
        here = pl.ds(j * quarter, quarter)
        for k in range(3):
            dilated[k, :, here] = held[m, k].T
        point[here, :] = held[m, 3]


def call(kernel, outs, args, specs, scratch, flops, limit, kept=pltpu.VMEM):
    nbytes = sum(a.size * a.dtype.itemsize for a in args) + sum(
        math.prod(s) * jnp.dtype(t).itemsize for s, t in outs
    )
    return pl.pallas_call(
        kernel,
        out_shape=[jax.ShapeDtypeStruct(s, t) for s, t in outs],
        in_specs=[pl.BlockSpec(memory_space=m) for m in specs],
        out_specs=[pl.BlockSpec(memory_space=kept)] * len(outs),
        scratch_shapes=scratch,
        compiler_params=pltpu.CompilerParams(vmem_limit_bytes=limit * MIB),
        cost_estimate=pl.CostEstimate(
            flops=flops, bytes_accessed=nbytes, transcendentals=0
        ),
    )(*args)


def local(inputs, norm_gain, dilated_weight, point_weight, cotangent):
    size = lax.axis_size("seq")
    depth = size // 4
    z, q = position()
    core = q % 2
    y = q // 2
    rows, channels = inputs.shape
    own = dilated_weight.shape[1]
    hidden = dilated_weight.shape[2]
    quarter = hidden // 4
    flops = 8 * rows * channels * quarter

    def send(value, target):
        pairs = [(i, target(i)) for i in range(size)]
        return lax.ppermute(
            value, "seq", [p for p in pairs if p[1] is not None and 0 <= p[1] < size]
        )

    def cross(value, m):
        return send(value, lambda i: i ^ m)

    def to_z(value, by):
        return send(value, lambda i: (i + 4 * by) % size)

    def cut(value, start, length, axis):
        return lax.dynamic_slice_in_dim(value, start, length, axis)

    def in_order(first, mine, other, axis):
        return jnp.where(
            first,
            jnp.concatenate([mine, other], axis),
            jnp.concatenate([other, mine], axis),
        )

    quarters = [
        cut(dilated_weight, toggled(q, m) * quarter, quarter, 2) for m in range(4)
    ]
    inputs = after(inputs, *quarters[1:])
    cotangent = after(cotangent, *quarters[1:])
    got = [quarters[0]] + [cross(quarters[m], m) for m in range(1, 4)]
    same = in_order(core == 0, got[0], got[1], 2)
    other = in_order(core == 0, got[2], got[3], 2)
    start_piece = in_order(y == 0, same[:, None], other[:, None], 1)

    def line(value, pairs):
        return lax.ppermute(
            value,
            "seq",
            [(4 * a + i, 4 * b + i) for a, b in pairs for i in range(4)],
        )

    if depth == 4:
        ups, downs = [start_piece], [start_piece]
        for j in range(3):
            ups.append(line(ups[-1], [(a, a + 1) for a in range(j, 3)]))
            downs.append(line(downs[-1], [(a + 1, a) for a in range(3 - j)]))
        pieces = ups + downs[1:]
    else:
        pieces = [start_piece] + [to_z(start_piece, d) for d in range(1, depth)]

    xfull = inputs.astype(f32)
    ratio = lax.rsqrt(jnp.mean(xfull * xfull, axis=-1, keepdims=True) + 1e-06)
    normed = xfull * ratio * norm_gain
    act = gelu_value(normed).astype(bf16)
    act_late = after(act, start_piece)
    cot_late = after(cotangent, start_piece)
    act_across = cross(act_late, 2)
    if depth == 4:
        act_across, pieces[1], pieces[4] = lax.optimization_barrier(
            (act_across, pieces[1], pieces[4])
        )
    edge = send(
        jnp.where(core == y, act_late, act_across),
        lambda i: i + 4 if i % 2 else i - 4,
    )
    edge_other = cross(edge, 1)
    cot_across = cross(after(cot_late, act_across), 2)
    acts = [act_late, cross(act_late, 1), act_across, cross(act_across, 1)]
    cots = [cot_late, cross(cot_late, 1), cot_across, cross(cot_across, 1)]
    point_rows = cut(point_weight, q * quarter, quarter, 0)

    width = channels // depth
    apart = width % 128 == 0
    outs = [
        ((4, quarter, width), t) for _, types in roles(depth, z) for t in types
    ]
    if not apart:
        outs = [((depth, 4, quarter, width), f32)]
    weight_outs = [((4 * rows, quarter), bf16)] * 2 + outs
    branch, pre_grad, *terms = call(
        functools.partial(weight_kernel, depth),
        weight_outs,
        [*pieces, *acts, edge, edge_other, *cots, point_rows],
        [pltpu.HBM] * (len(pieces) + 10) + [pltpu.VMEM],
        [
            pltpu.VMEM((6 * rows, channels), bf16),
            pltpu.VMEM((4 * rows, channels), bf16),
            pltpu.VMEM((3, depth, 2, own, 2 * quarter), bf16),
            pltpu.VMEM((3, channels, quarter), bf16),
            pltpu.VMEM((quarter, 4 * rows), bf16),
            pltpu.VMEM((quarter, 4 * rows), bf16),
            pltpu.VMEM((4 * rows, quarter), f32),
            pltpu.SemaphoreType.DMA((len(pieces) + 10 + len(weight_outs),)),
            *[pltpu.VMEM(*out) for out in weight_outs],
        ],
        8 * flops,
        60,
        pltpu.HBM,
    )
    if not apart:
        terms = [terms[0][d].astype(bf16) for d in range(1, depth)] + [terms[0][0]]
    if depth == 4:
        far, two, up, down, total = terms
        far = line(far, [(0, 1), (3, 2)])
        joined = (two + far.astype(f32)).astype(bf16)
        near_up = line(joined, [(0, 1), (1, 2)])
        near_down = line(joined, [(3, 2), (2, 1)])
        up = up + near_up.astype(f32)
        down = down + near_down.astype(f32)
        parts = [
            line(up.astype(bf16), [(0, 1), (1, 2), (2, 3)]),
            line(down.astype(bf16), [(1, 0), (2, 1), (3, 2)]),
        ]
    else:
        total = terms[-1]
        parts = [to_z(term, d + 1) for d, term in enumerate(terms[:-1])]

    grad_low = send(pre_grad[3 * rows :], lambda i: i + 4)
    grad_high = send(pre_grad[:rows], lambda i: i - 4)
    share_outs = [((rows, channels), t) for t in (f32, bf16, f32, bf16)]
    shares = call(
        functools.partial(backward_kernel, depth),
        share_outs,
        [*pieces, grad_low, pre_grad, grad_high],
        [pltpu.HBM] * (len(pieces) + 3),
        [
            pltpu.VMEM((6 * rows, quarter), bf16),
            pltpu.VMEM((3, depth, 2, own, 2 * quarter), bf16),
            pltpu.VMEM((3, channels, quarter), bf16),
            pltpu.SemaphoreType.DMA((len(pieces) + 7,)),
            *[pltpu.VMEM(*out) for out in share_outs],
        ],
        3 * flops,
        60,
        pltpu.HBM,
    )
    away = (shares[2] + cross(shares[3], 1).astype(f32)).astype(bf16)
    arrived = cross(away, 2)

    mine = shares[0] + cross(shares[1], 1).astype(f32)
    act_grad = mine + arrived.astype(f32)
    scaled = act_grad * gelu_slope(normed) * norm_gain
    inner = jnp.mean(scaled * xfull, axis=-1, keepdims=True)
    input_grad = (
        cotangent.astype(f32) + ratio * scaled - xfull * ratio * ratio * ratio * inner
    ).astype(bf16)

    branch = branch.reshape(2, 2, rows, quarter)
    keep = cut(branch, core, 1, 1)[:, 0]
    chip = in_order(core == 0, keep, cross(cut(branch, 1 - core, 1, 1)[:, 0], 1), 2)
    keep = cut(chip, y, 1, 0)[0]
    full = in_order(y == 0, keep, cross(cut(chip, 1 - y, 1, 0)[0], 2), 1)
    outputs = (xfull + product(full, point_weight)).astype(bf16)

    for part in parts:
        total = total + part.astype(f32)
    slices = [cut(total, toggled(q, m) * own, own, 2) for m in range(4)]
    slices = slices[:1] + [cross(slices[m].astype(bf16), m) for m in range(1, 4)]
    slices[3] = after(slices[3], input_grad, outputs)
    dilated_grad, point_grad = call(
        final_kernel,
        [((3, own, hidden), f32), ((hidden, own), f32)],
        slices,
        [pltpu.VMEM] * 4,
        [pltpu.VMEM((4, 4, quarter, own), f32)],
        1024,
        16,
    )
    return (outputs, input_grad, dilated_grad, point_grad)


def solution(mesh):
    placed = (
        P(("groups", "seq"), None),
        P(),
        P(None, "seq", None),
        P(),
        P(("groups", "seq"), None),
    )
    return jax.shard_map(
        local,
        mesh=mesh,
        in_specs=placed,
        out_specs=(
            P(("groups", "seq"), None),
            P(("groups", "seq"), None),
            P("groups", "seq", None),
            P("groups", "seq"),
        ),
        check_vma=False,
    )
```

```python
import functools
import math

import jax
import jax.numpy as jnp
from jax import lax
from jax.experimental import pallas as pl
from jax.experimental.pallas import tpu as pltpu
from jax.sharding import PartitionSpec as P

root_coef = math.sqrt(2.0 / math.pi)
bf16 = jnp.bfloat16
f32 = jnp.float32
MIB = 1024 * 1024


def gelu_value(v):
    return 0.5 * v * (1.0 + jnp.tanh(root_coef * (v + 0.044715 * v * v * v)))


def gelu_slope(v):
    inner = jnp.tanh(root_coef * (v + 0.044715 * v * v * v))
    return 0.5 * (1.0 + inner) + 0.5 * v * (1.0 - inner * inner) * root_coef * (
        1.0 + 3.0 * 0.044715 * v * v
    )


def after(value, *others):
    return lax.optimization_barrier((value, *others))[0]


def product(left, right):
    return jnp.dot(left, right, preferred_element_type=f32)


def transposed_product(left, weight):
    return lax.dot_general(
        left, weight, (((1,), (1,)), ((), ())), preferred_element_type=f32
    )


def position():
    me = lax.axis_index("seq")
    return me // 4, lax.rem(me, 4)


def toggled(q, bit):
    low = lax.rem(q, 2)
    if bit == 0:
        return q
    if bit == 1:
        return q + 1 - 2 * low
    if bit == 2:
        return lax.rem(q + 2, 4)
    return 3 - q


def within(start, length):
    return pl.ds(pl.multiple_of(start * length, length), length)


def started(pairs, sems, first=0):
    copies = []
    for i, (src, dst) in enumerate(pairs):
        sem = sems.at[first + i]
        if isinstance(src, tuple):
            chosen, src, other = src

            @pl.when(chosen)
            def _(src=src, dst=dst, sem=sem):
                pltpu.make_async_copy(src, dst, sem).start()

            @pl.when(jnp.logical_not(chosen))
            def _(src=other, dst=dst, sem=sem):
                pltpu.make_async_copy(src, dst, sem).start()

        else:
            pltpu.make_async_copy(src, dst, sem).start()
        copies.append(pltpu.make_async_copy(src, dst, sem))
    return copies


def finish(copies):
    for copy in copies:
        copy.wait()


def tap_pairs(depth, pieces, packed):
    z, _ = position()
    if depth == 4:
        own, *ups = pieces[:4]
        downs = pieces[4:]
        return [(own, packed.at[:, z])] + [
            ((z > j, ups[j], downs[2 - j]), packed.at[:, lax.rem(z + 3 - j, 4)])
            for j in range(3)
        ]
    return [
        (piece, packed.at[:, lax.rem(z + depth - d, depth)])
        for d, piece in enumerate(pieces)
    ]


def roles(depth, z):
    if depth == 4:
        return [
            (3 * lax.rem(z + 1, 2), [bf16, f32]),
            (lax.rem(z + 2, 4), [f32]),
            (1 + lax.rem(z, 2), [f32]),
            (z, [f32]),
        ]
    return [(lax.rem(z + d, depth), [bf16]) for d in range(1, depth)] + [(z, [f32])]


def unpack(packed, taps):
    _, depth, _, own, width = packed.shape
    quarter = width // 2
    _, q = position()
    y, core = (q // 2, lax.rem(q, 2)) if own % 16 == 0 else (0, 0)
    for i in range(2 * depth):
        side = y + (i % 2) * (1 - 2 * y)
        for half in range(2):
            start = 2 * (2 * (i // 2) + side) + core + half * (1 - 2 * core)
            here = within(start, own) if own % 16 == 0 else pl.ds(start * own, own)
            for k in range(3):
                taps[k, here, :] = packed[
                    k, i // 2, i % 2, :, half * quarter : (half + 1) * quarter
                ]


def weight_kernel(depth, *refs):
    count = depth + 3 * (depth == 4)
    pieces = refs[:count]
    acts = refs[count : count + 4]
    edge, edge_other = refs[count + 4 : count + 6]
    cots = refs[count + 6 : count + 10]
    point = refs[count + 10]
    refs = refs[count + 11 :]
    results = (len(refs) - 10) // 2
    low, high = refs[results : results + 2]
    refs = refs[:results] + refs[results + 2 :]
    stores, (wide, wide_cot, packed, taps, grads, branches, slopes, sems) = (
        refs[:results],
        refs[results : results + 8],
    )
    branch, grad, *outs = refs[results + 8 :]
    z, q = position()
    rows = acts[0].shape[0]
    core = lax.rem(q, 2)
    second = started(
        [(cot, wide_cot.at[within(toggled(q, m), rows)]) for m, cot in enumerate(cots)],
        sems,
    )
    first = started(
        [(act, wide.at[within(1 + toggled(q, m), rows)]) for m, act in enumerate(acts)]
        + [
            (edge, wide.at[within(5 * (1 - core), rows)]),
            (edge_other, wide.at[within(5 * core, rows)]),
        ]
        + tap_pairs(depth, pieces, packed),
        sems,
        len(second),
    )
    base = len(first) + len(second)
    finish(second)
    for part in range(4):
        here = pl.ds(part * rows, rows)
        slopes[here] = transposed_product(wide_cot[here], point[...])
    finish(first)
    unpack(packed, taps)
    for part in range(4):
        here = pl.ds(part * rows, rows)
        pre = product(wide[here], taps[0])
        pre = pre + product(wide[pl.ds((part + 1) * rows, rows)], taps[1])
        pre = pre + product(wide[pl.ds((part + 2) * rows, rows)], taps[2])
        value = gelu_value(pre)
        branch[here] = value.astype(bf16)
        branches[:, here] = value.T.astype(bf16)
        value = slopes[here] * gelu_slope(pre)
        grad[here] = value.astype(bf16)
        grads[:, here] = value.T.astype(bf16)
    last = started([(grad, stores[1]), (branch, stores[0])], sems, base)
    ends = [(grad.at[pl.ds(3 * rows, rows)], low), (grad.at[pl.ds(0, rows)], high)]
    last += started(ends, sems, base + len(stores))
    width = wide.shape[1] // depth
    if len(outs) == 1:
        for i in range(depth):
            lanes = pl.ds(i * width, width)
            out = outs[0].at[lax.rem(i + depth - z, depth)]
            for k in range(3):
                out[k] = product(grads[...], wide[pl.ds(k * rows, 4 * rows), lanes])
            out[3] = product(branches[...], wide_cot[:, lanes])
        last += started([(outs[0], stores[2])], sems, base + 2)
    else:
        i = 0
        for target, types in roles(depth, z):
            lanes = within(target, width)
            same = outs[i : i + len(types)]
            for k in range(4):
                if k < 3:
                    value = product(
                        grads[...], wide[pl.ds(k * rows, 4 * rows), lanes]
                    )
                else:
                    value = product(branches[...], wide_cot[:, lanes])
                for out in same:
                    out[k] = value.astype(out.dtype)
            i += len(types)
            if depth != 4:
                last += started([(same[0], stores[1 + i])], sems, base + 1 + i)
            elif i == 2:
                last += started([(outs[0], stores[2])], sems, base + 2)
            elif i == 3:
                last += started([(outs[2], stores[3])], sems, base + 3)
            elif i == 4:
                last += started(
                    [
                        ((z == 2, outs[1], outs[3]), stores[4]),
                        ((z == 1, outs[1], outs[3]), stores[5]),
                    ],
                    sems,
                    base + 4,
                )
            else:
                last += started([(outs[4], stores[6])], sems, base + 6)
    finish(last)


def backward_kernel(depth, *refs):
    count = depth + 3 * (depth == 4)
    pieces = refs[:count]
    low, grad, high = refs[count : count + 3]
    stores = refs[count + 3 : count + 7]
    wide, packed, taps, sems = refs[count + 7 : count + 11]
    outs = refs[count + 11 :]
    _, q = position()
    rows = low.shape[0]
    finish(
        started(
            [
                (low, wide.at[pl.ds(0, rows)]),
                (grad, wide.at[pl.ds(rows, 4 * rows)]),
                (high, wide.at[pl.ds(5 * rows, rows)]),
            ]
            + tap_pairs(depth, pieces, packed),
            sems,
        )
    )
    unpack(packed, taps)
    last = []
    for m in (1, 3, 2, 0):
        part = toggled(q, m)
        total = None
        for k in range(3):
            term = transposed_product(wide[within(part + 2 - k, rows)], taps[k])
            total = term if total is None else total + term
        outs[m][...] = total.astype(outs[m].dtype)
        last += started([(outs[m], stores[m])], sems, count + 3 + m)
    finish(last)


def final_kernel(*refs):
    parts = refs[:4]
    dilated, point, held = refs[4:]
    _, q = position()
    quarter = parts[0].shape[1]
    for m in range(4):
        held[m] = parts[m][...].astype(f32)
    for j in range(4):
        m = lax.rem(q + j, 2) + 2 * lax.rem(q // 2 + j // 2, 2)
        here = pl.ds(j * quarter, quarter)
        for k in range(3):
            dilated[k, :, here] = held[m, k].T
        point[:, here] = held[m, 3].T


def call(kernel, outs, args, specs, scratch, flops, limit, kept=pltpu.VMEM):
    nbytes = sum(a.size * a.dtype.itemsize for a in args) + sum(
        math.prod(s) * jnp.dtype(t).itemsize for s, t in outs
    )
    return pl.pallas_call(
        kernel,
        out_shape=[jax.ShapeDtypeStruct(s, t) for s, t in outs],
        in_specs=[pl.BlockSpec(memory_space=m) for m in specs],
        out_specs=[pl.BlockSpec(memory_space=kept)] * len(outs),
        scratch_shapes=scratch,
        compiler_params=pltpu.CompilerParams(vmem_limit_bytes=limit * MIB),
        cost_estimate=pl.CostEstimate(
            flops=flops, bytes_accessed=nbytes, transcendentals=0
        ),
    )(*args)


def local(inputs, norm_gain, dilated_weight, point_weight, cotangent):
    size = lax.axis_size("seq")
    depth = size // 4
    z, q = position()
    core = q % 2
    y = q // 2
    rows, channels = inputs.shape
    own = dilated_weight.shape[1]
    hidden = dilated_weight.shape[2]
    quarter = hidden // 4
    flops = 8 * rows * channels * quarter

    def send(value, target):
        pairs = [(i, target(i)) for i in range(size)]
        return lax.ppermute(
            value, "seq", [p for p in pairs if p[1] is not None and 0 <= p[1] < size]
        )

    def cross(value, m):
        return send(value, lambda i: i ^ m)

    def to_z(value, by):
        return send(value, lambda i: (i + 4 * by) % size)

    def cut(value, start, length, axis):
        return lax.dynamic_slice_in_dim(value, start, length, axis)

    def in_order(first, mine, other, axis):
        return jnp.where(
            first,
            jnp.concatenate([mine, other], axis),
            jnp.concatenate([other, mine], axis),
        )

    quarters = [
        cut(dilated_weight, toggled(q, m) * quarter, quarter, 2) for m in range(4)
    ]
    inputs = after(inputs, *quarters[1:])
    cotangent = after(cotangent, *quarters[1:])
    got = [quarters[0]] + [cross(quarters[m], m) for m in range(1, 4)]
    if own % 16 == 0:
        same = jnp.concatenate(got[:2], 2)
        other = jnp.concatenate(got[2:], 2)
        start_piece = jnp.stack([same, other], 1)
    else:
        same = in_order(core == 0, got[0], got[1], 2)
        other = in_order(core == 0, got[2], got[3], 2)
        start_piece = in_order(y == 0, same[:, None], other[:, None], 1)

    def line(value, pairs):
        return lax.ppermute(
            value,
            "seq",
            [(4 * a + i, 4 * b + i) for a, b in pairs for i in range(4)],
        )

    if depth == 4:
        ups, downs = [start_piece], [start_piece]
        for j in range(3):
            ups.append(line(ups[-1], [(a, a + 1) for a in range(j, 3)]))
            downs.append(line(downs[-1], [(a + 1, a) for a in range(3 - j)]))
        pieces = ups + downs[1:]
    else:
        pieces = [start_piece] + [to_z(start_piece, d) for d in range(1, depth)]

    xfull = inputs.astype(f32)
    ratio = lax.rsqrt(jnp.mean(xfull * xfull, axis=-1, keepdims=True) + 1e-06)
    normed = xfull * ratio * norm_gain
    act = gelu_value(normed).astype(bf16)
    act_late = after(act, start_piece)
    cot_late = after(cotangent, start_piece)
    act_across = cross(act_late, 2)
    if depth == 4:
        act_across, pieces[1], pieces[4] = lax.optimization_barrier(
            (act_across, pieces[1], pieces[4])
        )
    edge = send(
        jnp.where(core == y, act_late, act_across),
        lambda i: i + 4 if i % 2 else i - 4,
    )
    edge_other = cross(edge, 1)
    cot_across = cross(after(cot_late, act_across), 2)
    acts = [act_late, cross(act_late, 1), act_across, cross(act_across, 1)]
    cots = [cot_late, cross(cot_late, 1), cot_across, cross(cot_across, 1)]
    point_rows = cut(point_weight, q * quarter, quarter, 0)

    width = channels // depth
    apart = width % 128 == 0
    outs = [
        ((4, quarter, width), t) for _, types in roles(depth, z) for t in types
    ]
    if not apart:
        outs = [((depth, 4, quarter, width), f32)]
    weight_outs = [((4 * rows, quarter), bf16)] * 2 + outs
    *terms, low, high = call(
        functools.partial(weight_kernel, depth),
        weight_outs + [((rows, quarter), bf16)] * 2,
        [*pieces, *acts, edge, edge_other, *cots, point_rows],
        [pltpu.HBM] * (len(pieces) + 10) + [pltpu.VMEM],
        [
            pltpu.VMEM((6 * rows, channels), bf16),
            pltpu.VMEM((4 * rows, channels), bf16),
            pltpu.VMEM((3, depth, 2, own, 2 * quarter), bf16),
            pltpu.VMEM((3, channels, quarter), bf16),
            pltpu.VMEM((quarter, 4 * rows), bf16),
            pltpu.VMEM((quarter, 4 * rows), bf16),
            pltpu.VMEM((4 * rows, quarter), f32),
            pltpu.SemaphoreType.DMA((len(pieces) + 12 + len(weight_outs),)),
            *[pltpu.VMEM(*out) for out in weight_outs],
        ],
        8 * flops,
        60,
        pltpu.HBM,
    )
    branch, pre_grad, *terms = terms
    if not apart:
        terms = [terms[0][d].astype(bf16) for d in range(1, depth)] + [terms[0][0]]
    if depth == 4:
        far, two, up, down, total = terms
        far = line(far, [(0, 1), (3, 2)])
        joined = (two + far.astype(f32)).astype(bf16)
        near_up = line(joined, [(0, 1), (1, 2)])
        near_down = line(joined, [(3, 2), (2, 1)])
        up = up + near_up.astype(f32)
        down = down + near_down.astype(f32)
        parts = [
            line(up.astype(bf16), [(0, 1), (1, 2), (2, 3)]),
            line(down.astype(bf16), [(1, 0), (2, 1), (3, 2)]),
        ]
    else:
        total = terms[-1]
        parts = [to_z(term, d + 1) for d, term in enumerate(terms[:-1])]

    grad_low = send(low, lambda i: i + 4)
    grad_high = send(high, lambda i: i - 4)
    share_outs = [((rows, channels), t) for t in (f32, bf16, f32, bf16)]
    shares = call(
        functools.partial(backward_kernel, depth),
        share_outs,
        [*pieces, grad_low, pre_grad, grad_high],
        [pltpu.HBM] * (len(pieces) + 3),
        [
            pltpu.VMEM((6 * rows, quarter), bf16),
            pltpu.VMEM((3, depth, 2, own, 2 * quarter), bf16),
            pltpu.VMEM((3, channels, quarter), bf16),
            pltpu.SemaphoreType.DMA((len(pieces) + 7,)),
            *[pltpu.VMEM(*out) for out in share_outs],
        ],
        3 * flops,
        60,
        pltpu.HBM,
    )
    away = (shares[2] + cross(shares[3], 1).astype(f32)).astype(bf16)
    arrived = cross(away, 2)

    mine = shares[0] + cross(shares[1], 1).astype(f32)
    act_grad = mine + arrived.astype(f32)
    scaled = act_grad * gelu_slope(normed) * norm_gain
    inner = jnp.mean(scaled * xfull, axis=-1, keepdims=True)
    input_grad = (
        cotangent.astype(f32) + ratio * scaled - xfull * ratio * ratio * ratio * inner
    ).astype(bf16)

    branch = branch.reshape(2, 2, rows, quarter)
    keep = cut(branch, core, 1, 1)[:, 0]
    chip = in_order(core == 0, keep, cross(cut(branch, 1 - core, 1, 1)[:, 0], 1), 2)
    keep = cut(chip, y, 1, 0)[0]
    full = in_order(y == 0, keep, cross(cut(chip, 1 - y, 1, 0)[0], 2), 1)
    outputs = (xfull + product(full, point_weight)).astype(bf16)

    for part in parts:
        total = total + part.astype(f32)
    slices = [cut(total, toggled(q, m) * own, own, 2) for m in range(4)]
    slices = slices[:1] + [cross(slices[m].astype(bf16), m) for m in range(1, 4)]
    slices[3] = after(slices[3], input_grad, outputs)
    dilated_grad, point_grad = call(
        final_kernel,
        [((3, own, hidden), f32), ((own, hidden), f32)],
        slices,
        [pltpu.VMEM] * 4,
        [pltpu.VMEM((4, 4, quarter, own), f32)],
        1024,
        16,
    )
    return (outputs, input_grad, dilated_grad, point_grad.T)


def solution(mesh):
    placed = (
        P(("groups", "seq"), None),
        P(),
        P(None, "seq", None),
        P(),
        P(("groups", "seq"), None),
    )
    return jax.shard_map(
        local,
        mesh=mesh,
        in_specs=placed,
        out_specs=(
            P(("groups", "seq"), None),
            P(("groups", "seq"), None),
            P("groups", "seq", None),
            P("groups", "seq"),
        ),
        check_vma=False,
    )
```

```python
import functools
import math

import jax
import jax.numpy as jnp
from jax import lax
from jax.experimental import pallas as pl
from jax.experimental.pallas import tpu as pltpu
from jax.sharding import PartitionSpec as P

root_coef = math.sqrt(2.0 / math.pi)
bf16 = jnp.bfloat16
f32 = jnp.float32
MIB = 1024 * 1024


def gelu_value(v):
    return 0.5 * v * (1.0 + jnp.tanh(root_coef * (v + 0.044715 * v * v * v)))


def gelu_slope(v):
    inner = jnp.tanh(root_coef * (v + 0.044715 * v * v * v))
    return 0.5 * (1.0 + inner) + 0.5 * v * (1.0 - inner * inner) * root_coef * (
        1.0 + 3.0 * 0.044715 * v * v
    )


def after(value, *others):
    return lax.optimization_barrier((value, *others))[0]


def product(left, right):
    return jnp.dot(left, right, preferred_element_type=f32)


def transposed_product(left, weight):
    return lax.dot_general(
        left, weight, (((1,), (1,)), ((), ())), preferred_element_type=f32
    )


def position():
    me = lax.axis_index("seq")
    return me // 4, lax.rem(me, 4)


def toggled(q, bit):
    low = lax.rem(q, 2)
    if bit == 0:
        return q
    if bit == 1:
        return q + 1 - 2 * low
    if bit == 2:
        return lax.rem(q + 2, 4)
    return 3 - q


def within(start, length):
    return pl.ds(pl.multiple_of(start * length, length), length)


def started(pairs, sems, first=0):
    copies = []
    for i, (src, dst) in enumerate(pairs):
        sem = sems.at[first + i]
        if isinstance(src, tuple):
            chosen, src, other = src

            @pl.when(chosen)
            def _(src=src, dst=dst, sem=sem):
                pltpu.make_async_copy(src, dst, sem).start()

            @pl.when(jnp.logical_not(chosen))
            def _(src=other, dst=dst, sem=sem):
                pltpu.make_async_copy(src, dst, sem).start()

        else:
            pltpu.make_async_copy(src, dst, sem).start()
        copies.append(pltpu.make_async_copy(src, dst, sem))
    return copies


def finish(copies):
    for copy in copies:
        copy.wait()


def tap_pairs(depth, pieces, packed):
    z, _ = position()
    if depth == 4:
        own, *ups = pieces[:4]
        downs = pieces[4:]
        return [(own, packed.at[:, z])] + [
            ((z > j, ups[j], downs[2 - j]), packed.at[:, lax.rem(z + 3 - j, 4)])
            for j in range(3)
        ]
    return [
        (piece, packed.at[:, lax.rem(z + depth - d, depth)])
        for d, piece in enumerate(pieces)
    ]


def roles(depth, z):
    if depth == 4:
        return [
            (3 * lax.rem(z + 1, 2), [bf16, bf16]),
            (lax.rem(z + 2, 4), [bf16]),
            (1 + lax.rem(z, 2), [bf16]),
            (z, [f32]),
        ]
    return [(lax.rem(z + d, depth), [bf16]) for d in range(1, depth)] + [(z, [f32])]


def unpack(packed, taps):
    _, depth, _, own, width = packed.shape
    quarter = width // 2
    _, q = position()
    y, core = (q // 2, lax.rem(q, 2)) if own % 16 == 0 else (0, 0)
    for i in range(2 * depth):
        side = y + (i % 2) * (1 - 2 * y)
        for half in range(2):
            start = 2 * (2 * (i // 2) + side) + core + half * (1 - 2 * core)
            here = within(start, own) if own % 16 == 0 else pl.ds(start * own, own)
            for k in range(3):
                taps[k, here, :] = packed[
                    k, i // 2, i % 2, :, half * quarter : (half + 1) * quarter
                ]


def weight_kernel(depth, *refs):
    count = depth + 3 * (depth == 4)
    pieces = refs[:count]
    acts = refs[count : count + 4]
    edge, edge_other = refs[count + 4 : count + 6]
    cots = refs[count + 6 : count + 10]
    point = refs[count + 10]
    refs = refs[count + 11 :]
    results = (len(refs) - 10) // 2
    low, high = refs[results : results + 2]
    refs = refs[:results] + refs[results + 2 :]
    stores, (wide, wide_cot, packed, taps, grads, branches, slopes, sems) = (
        refs[:results],
        refs[results : results + 8],
    )
    branch, grad, *outs = refs[results + 8 :]
    z, q = position()
    rows = acts[0].shape[0]
    core = lax.rem(q, 2)
    second = started(
        [(cot, wide_cot.at[within(toggled(q, m), rows)]) for m, cot in enumerate(cots)],
        sems,
    )
    first = started(
        [(act, wide.at[within(1 + toggled(q, m), rows)]) for m, act in enumerate(acts)]
        + [
            (edge, wide.at[within(5 * (1 - core), rows)]),
            (edge_other, wide.at[within(5 * core, rows)]),
        ]
        + tap_pairs(depth, pieces, packed),
        sems,
        len(second),
    )
    base = len(first) + len(second)
    finish(second)
    for part in range(4):
        here = pl.ds(part * rows, rows)
        slopes[here] = transposed_product(wide_cot[here], point[...])
    finish(first)
    unpack(packed, taps)
    for part in range(4):
        here = pl.ds(part * rows, rows)
        pre = product(wide[here], taps[0])
        pre = pre + product(wide[pl.ds((part + 1) * rows, rows)], taps[1])
        pre = pre + product(wide[pl.ds((part + 2) * rows, rows)], taps[2])
        value = gelu_value(pre)
        branch[here] = value.astype(bf16)
        branches[:, here] = value.T.astype(bf16)
        value = slopes[here] * gelu_slope(pre)
        grad[here] = value.astype(bf16)
        grads[:, here] = value.T.astype(bf16)
    last = started([(grad, stores[1]), (branch, stores[0])], sems, base)
    ends = [(grad.at[pl.ds(3 * rows, rows)], low), (grad.at[pl.ds(0, rows)], high)]
    last += started(ends, sems, base + len(stores))
    width = wide.shape[1] // depth
    if len(outs) == 1:
        for i in range(depth):
            lanes = pl.ds(i * width, width)
            out = outs[0].at[lax.rem(i + depth - z, depth)]
            for k in range(3):
                out[k] = product(grads[...], wide[pl.ds(k * rows, 4 * rows), lanes])
            out[3] = product(branches[...], wide_cot[:, lanes])
        last += started([(outs[0], stores[2])], sems, base + 2)
    else:
        i = 0
        for target, types in roles(depth, z):
            lanes = within(target, width)
            same = outs[i : i + len(types)]
            for k in range(4):
                if k < 3:
                    value = product(
                        grads[...], wide[pl.ds(k * rows, 4 * rows), lanes]
                    )
                else:
                    value = product(branches[...], wide_cot[:, lanes])
                for out in same:
                    out[k] = value.astype(out.dtype)
            i += len(types)
            if depth != 4:
                last += started([(same[0], stores[1 + i])], sems, base + 1 + i)
            elif i == 2:
                last += started([(outs[0], stores[2])], sems, base + 2)
            elif i == 3:
                last += started([(outs[2], stores[3])], sems, base + 3)
            elif i == 4:
                last += started(
                    [
                        ((z == 2, outs[1], outs[3]), stores[4]),
                        ((z == 1, outs[1], outs[3]), stores[5]),
                    ],
                    sems,
                    base + 4,
                )
            else:
                last += started([(outs[4], stores[6])], sems, base + 6)
    finish(last)


def backward_kernel(depth, *refs):
    count = depth + 3 * (depth == 4)
    pieces = refs[:count]
    low, grad, high = refs[count : count + 3]
    stores = refs[count + 3 : count + 7]
    wide, packed, taps, sems = refs[count + 7 : count + 11]
    outs = refs[count + 11 :]
    _, q = position()
    rows = low.shape[0]
    finish(
        started(
            [
                (low, wide.at[pl.ds(0, rows)]),
                (grad, wide.at[pl.ds(rows, 4 * rows)]),
                (high, wide.at[pl.ds(5 * rows, rows)]),
            ]
            + tap_pairs(depth, pieces, packed),
            sems,
        )
    )
    unpack(packed, taps)
    last = []
    for m in (1, 3, 2, 0):
        part = toggled(q, m)
        total = None
        for k in range(3):
            term = transposed_product(wide[within(part + 2 - k, rows)], taps[k])
            total = term if total is None else total + term
        outs[m][...] = total.astype(outs[m].dtype)
        last += started([(outs[m], stores[m])], sems, count + 3 + m)
    finish(last)


def final_kernel(*refs):
    parts = refs[:4]
    dilated, point, held = refs[4:]
    _, q = position()
    quarter = parts[0].shape[1]
    for m in range(4):
        held[m] = parts[m][...].astype(f32)
    for j in range(4):
        m = lax.rem(q + j, 2) + 2 * lax.rem(q // 2 + j // 2, 2)
        here = pl.ds(j * quarter, quarter)
        for k in range(3):
            dilated[k, :, here] = held[m, k].T
        point[:, here] = held[m, 3].T


def call(kernel, outs, args, specs, scratch, flops, limit, kept=pltpu.VMEM):
    nbytes = sum(a.size * a.dtype.itemsize for a in args) + sum(
        math.prod(s) * jnp.dtype(t).itemsize for s, t in outs
    )
    return pl.pallas_call(
        kernel,
        out_shape=[jax.ShapeDtypeStruct(s, t) for s, t in outs],
        in_specs=[pl.BlockSpec(memory_space=m) for m in specs],
        out_specs=[pl.BlockSpec(memory_space=kept)] * len(outs),
        scratch_shapes=scratch,
        compiler_params=pltpu.CompilerParams(vmem_limit_bytes=limit * MIB),
        cost_estimate=pl.CostEstimate(
            flops=flops, bytes_accessed=nbytes, transcendentals=0
        ),
    )(*args)


def local(inputs, norm_gain, dilated_weight, point_weight, cotangent):
    size = lax.axis_size("seq")
    depth = size // 4
    z, q = position()
    core = q % 2
    y = q // 2
    rows, channels = inputs.shape
    own = dilated_weight.shape[1]
    hidden = dilated_weight.shape[2]
    quarter = hidden // 4
    flops = 8 * rows * channels * quarter

    def send(value, target):
        pairs = [(i, target(i)) for i in range(size)]
        return lax.ppermute(
            value, "seq", [p for p in pairs if p[1] is not None and 0 <= p[1] < size]
        )

    def cross(value, m):
        return send(value, lambda i: i ^ m)

    def to_z(value, by):
        return send(value, lambda i: (i + 4 * by) % size)

    def cut(value, start, length, axis):
        return lax.dynamic_slice_in_dim(value, start, length, axis)

    def in_order(first, mine, other, axis):
        return jnp.where(
            first,
            jnp.concatenate([mine, other], axis),
            jnp.concatenate([other, mine], axis),
        )

    quarters = [
        cut(dilated_weight, toggled(q, m) * quarter, quarter, 2) for m in range(4)
    ]
    inputs = after(inputs, *quarters[1:])
    cotangent = after(cotangent, *quarters[1:])
    got = [quarters[0]] + [cross(quarters[m], m) for m in range(1, 4)]
    if own % 16 == 0:
        same = jnp.concatenate(got[:2], 2)
        other = jnp.concatenate(got[2:], 2)
        start_piece = jnp.stack([same, other], 1)
    else:
        same = in_order(core == 0, got[0], got[1], 2)
        other = in_order(core == 0, got[2], got[3], 2)
        start_piece = in_order(y == 0, same[:, None], other[:, None], 1)

    def line(value, pairs):
        return lax.ppermute(
            value,
            "seq",
            [(4 * a + i, 4 * b + i) for a, b in pairs for i in range(4)],
        )

    if depth == 4:
        ups, downs = [start_piece], [start_piece]
        for j in range(3):
            ups.append(line(ups[-1], [(a, a + 1) for a in range(j, 3)]))
            downs.append(line(downs[-1], [(a + 1, a) for a in range(3 - j)]))
        pieces = ups + downs[1:]
    else:
        pieces = [start_piece] + [to_z(start_piece, d) for d in range(1, depth)]

    xfull = inputs.astype(f32)
    ratio = lax.rsqrt(jnp.mean(xfull * xfull, axis=-1, keepdims=True) + 1e-06)
    normed = xfull * ratio * norm_gain
    act = gelu_value(normed).astype(bf16)
    act_late = after(act, start_piece)
    cot_late = after(cotangent, start_piece)
    act_across = cross(act_late, 2)
    if depth == 4:
        act_across, pieces[1], pieces[4] = lax.optimization_barrier(
            (act_across, pieces[1], pieces[4])
        )
    edge = send(
        jnp.where(core == y, act_late, act_across),
        lambda i: i + 4 if i % 2 else i - 4,
    )
    edge_other = cross(edge, 1)
    cot_across = cross(after(cot_late, act_across), 2)
    acts = [act_late, cross(act_late, 1), act_across, cross(act_across, 1)]
    cots = [cot_late, cross(cot_late, 1), cot_across, cross(cot_across, 1)]
    point_rows = cut(point_weight, q * quarter, quarter, 0)

    width = channels // depth
    apart = width % 128 == 0
    outs = [
        ((4, quarter, width), t) for _, types in roles(depth, z) for t in types
    ]
    if not apart:
        outs = [((depth, 4, quarter, width), f32)]
    weight_outs = [((4 * rows, quarter), bf16)] * 2 + outs
    *terms, low, high = call(
        functools.partial(weight_kernel, depth),
        weight_outs + [((rows, quarter), bf16)] * 2,
        [*pieces, *acts, edge, edge_other, *cots, point_rows],
        [pltpu.HBM] * (len(pieces) + 10) + [pltpu.VMEM],
        [
            pltpu.VMEM((6 * rows, channels), bf16),
            pltpu.VMEM((4 * rows, channels), bf16),
            pltpu.VMEM((3, depth, 2, own, 2 * quarter), bf16),
            pltpu.VMEM((3, channels, quarter), bf16),
            pltpu.VMEM((quarter, 4 * rows), bf16),
            pltpu.VMEM((quarter, 4 * rows), bf16),
            pltpu.VMEM((4 * rows, quarter), f32),
            pltpu.SemaphoreType.DMA((len(pieces) + 12 + len(weight_outs),)),
            *[pltpu.VMEM(*out) for out in weight_outs],
        ],
        8 * flops,
        60,
        pltpu.HBM,
    )
    branch, pre_grad, *terms = terms
    if not apart:
        terms = [terms[0][d].astype(bf16) for d in range(1, depth)] + [terms[0][0]]
    if depth == 4:
        far, two, up, down, total = terms
        far = line(far, [(0, 1), (3, 2)])
        joined = (two.astype(f32) + far.astype(f32)).astype(bf16)
        near_up = line(joined, [(0, 1), (1, 2)])
        near_down = line(joined, [(3, 2), (2, 1)])
        up = up.astype(f32) + near_up.astype(f32)
        down = down.astype(f32) + near_down.astype(f32)
        parts = [
            line(up.astype(bf16), [(0, 1), (1, 2), (2, 3)]),
            line(down.astype(bf16), [(1, 0), (2, 1), (3, 2)]),
        ]
    else:
        total = terms[-1]
        parts = [to_z(term, d + 1) for d, term in enumerate(terms[:-1])]

    grad_low = send(low, lambda i: i + 4)
    grad_high = send(high, lambda i: i - 4)
    share_outs = [((rows, channels), t) for t in (f32, bf16, f32, bf16)]
    shares = call(
        functools.partial(backward_kernel, depth),
        share_outs,
        [*pieces, grad_low, pre_grad, grad_high],
        [pltpu.HBM] * (len(pieces) + 3),
        [
            pltpu.VMEM((6 * rows, quarter), bf16),
            pltpu.VMEM((3, depth, 2, own, 2 * quarter), bf16),
            pltpu.VMEM((3, channels, quarter), bf16),
            pltpu.SemaphoreType.DMA((len(pieces) + 7,)),
            *[pltpu.VMEM(*out) for out in share_outs],
        ],
        3 * flops,
        60,
        pltpu.HBM,
    )
    away = (shares[2] + cross(shares[3], 1).astype(f32)).astype(bf16)
    arrived = cross(away, 2)

    mine = shares[0] + cross(shares[1], 1).astype(f32)
    act_grad = mine + arrived.astype(f32)
    scaled = act_grad * gelu_slope(normed) * norm_gain
    inner = jnp.mean(scaled * xfull, axis=-1, keepdims=True)
    input_grad = (
        cotangent.astype(f32) + ratio * scaled - xfull * ratio * ratio * ratio * inner
    ).astype(bf16)

    branch = branch.reshape(2, 2, rows, quarter)
    keep = cut(branch, core, 1, 1)[:, 0]
    chip = in_order(core == 0, keep, cross(cut(branch, 1 - core, 1, 1)[:, 0], 1), 2)
    keep = cut(chip, y, 1, 0)[0]
    full = in_order(y == 0, keep, cross(cut(chip, 1 - y, 1, 0)[0], 2), 1)
    outputs = (xfull + product(full, point_weight)).astype(bf16)

    for part in parts:
        total = total + part.astype(f32)
    slices = [cut(total, toggled(q, m) * own, own, 2) for m in range(4)]
    slices = slices[:1] + [cross(slices[m].astype(bf16), m) for m in range(1, 4)]
    slices[3] = after(slices[3], input_grad, outputs)
    dilated_grad, point_grad = call(
        final_kernel,
        [((3, own, hidden), f32), ((own, hidden), f32)],
        slices,
        [pltpu.VMEM] * 4,
        [pltpu.VMEM((4, 4, quarter, own), f32)],
        1024,
        16,
    )
    return (outputs, input_grad, dilated_grad, point_grad.T)


def solution(mesh):
    placed = (
        P(("groups", "seq"), None),
        P(),
        P(None, "seq", None),
        P(),
        P(("groups", "seq"), None),
    )
    return jax.shard_map(
        local,
        mesh=mesh,
        in_specs=placed,
        out_specs=(
            P(("groups", "seq"), None),
            P(("groups", "seq"), None),
            P("groups", "seq", None),
            P("groups", "seq"),
        ),
        check_vma=False,
    )
```

```python
import functools
import math

import jax
import jax.numpy as jnp
from jax import lax
from jax.experimental import pallas as pl
from jax.experimental.pallas import tpu as pltpu
from jax.sharding import PartitionSpec as P

root_coef = math.sqrt(2.0 / math.pi)
bf16 = jnp.bfloat16
f32 = jnp.float32
MIB = 1024 * 1024


def gelu_value(v):
    return 0.5 * v * (1.0 + jnp.tanh(root_coef * (v + 0.044715 * v * v * v)))


def gelu_slope(v):
    inner = jnp.tanh(root_coef * (v + 0.044715 * v * v * v))
    return 0.5 * (1.0 + inner) + 0.5 * v * (1.0 - inner * inner) * root_coef * (
        1.0 + 3.0 * 0.044715 * v * v
    )


def after(value, *others):
    return lax.optimization_barrier((value, *others))[0]


def product(left, right):
    return jnp.dot(left, right, preferred_element_type=f32)


def transposed_product(left, weight):
    return lax.dot_general(
        left, weight, (((1,), (1,)), ((), ())), preferred_element_type=f32
    )


def position():
    me = lax.axis_index("seq")
    return me // 4, lax.rem(me, 4)


def toggled(q, bit):
    low = lax.rem(q, 2)
    if bit == 0:
        return q
    if bit == 1:
        return q + 1 - 2 * low
    if bit == 2:
        return lax.rem(q + 2, 4)
    return 3 - q


def within(start, length):
    return pl.ds(pl.multiple_of(start * length, length), length)


def started(pairs, sems, first=0):
    copies = []
    for i, (src, dst) in enumerate(pairs):
        sem = sems.at[first + i]
        if isinstance(src, tuple):
            chosen, src, other = src

            @pl.when(chosen)
            def _(src=src, dst=dst, sem=sem):
                pltpu.make_async_copy(src, dst, sem).start()

            @pl.when(jnp.logical_not(chosen))
            def _(src=other, dst=dst, sem=sem):
                pltpu.make_async_copy(src, dst, sem).start()

        else:
            pltpu.make_async_copy(src, dst, sem).start()
        copies.append(pltpu.make_async_copy(src, dst, sem))
    return copies


def finish(copies):
    for copy in copies:
        copy.wait()


def tap_pairs(depth, pieces, packed):
    z, _ = position()
    if depth == 4:
        own, *ups = pieces[:4]
        downs = pieces[4:]
        return [(own, packed.at[:, z])] + [
            ((z > j, ups[j], downs[2 - j]), packed.at[:, lax.rem(z + 3 - j, 4)])
            for j in range(3)
        ]
    return [
        (piece, packed.at[:, lax.rem(z + depth - d, depth)])
        for d, piece in enumerate(pieces)
    ]


def roles(depth, z):
    if depth == 4:
        return [
            (3 * lax.rem(z + 1, 2), [bf16, f32]),
            (lax.rem(z + 2, 4), [f32]),
            (1 + lax.rem(z, 2), [f32]),
            (z, [f32]),
        ]
    return [(lax.rem(z + d, depth), [bf16]) for d in range(1, depth)] + [(z, [f32])]


def unpack(packed, taps):
    _, depth, _, own, width = packed.shape
    quarter = width // 2
    _, q = position()
    y, core = (q // 2, lax.rem(q, 2)) if own % 16 == 0 else (0, 0)
    for i in range(2 * depth):
        side = y + (i % 2) * (1 - 2 * y)
        for half in range(2):
            start = 2 * (2 * (i // 2) + side) + core + half * (1 - 2 * core)
            here = within(start, own) if own % 16 == 0 else pl.ds(start * own, own)
            for k in range(3):
                taps[k, here, :] = packed[
                    k, i // 2, i % 2, :, half * quarter : (half + 1) * quarter
                ]


def weight_kernel(depth, *refs):
    count = depth + 3 * (depth == 4)
    pieces = refs[:count]
    acts = refs[count : count + 4]
    edge, edge_other = refs[count + 4 : count + 6]
    cots = refs[count + 6 : count + 10]
    point = refs[count + 10]
    refs = refs[count + 11 :]
    results = (len(refs) - 10) // 2
    low, high = refs[results : results + 2]
    refs = refs[:results] + refs[results + 2 :]
    stores, (wide, wide_cot, packed, taps, grads, branches, slopes, sems) = (
        refs[:results],
        refs[results : results + 8],
    )
    branch, grad, *outs = refs[results + 8 :]
    z, q = position()
    rows = acts[0].shape[0]
    core = lax.rem(q, 2)
    second = started(
        [(cot, wide_cot.at[within(toggled(q, m), rows)]) for m, cot in enumerate(cots)],
        sems,
    )
    first = started(
        [(act, wide.at[within(1 + toggled(q, m), rows)]) for m, act in enumerate(acts)]
        + [
            (edge, wide.at[within(5 * (1 - core), rows)]),
            (edge_other, wide.at[within(5 * core, rows)]),
        ]
        + tap_pairs(depth, pieces, packed),
        sems,
        len(second),
    )
    base = len(first) + len(second)
    finish(second)
    for part in range(4):
        here = pl.ds(part * rows, rows)
        slopes[here] = transposed_product(wide_cot[here], point[...])
    finish(first)
    unpack(packed, taps)
    for part in range(4):
        here = pl.ds(part * rows, rows)
        pre = product(wide[here], taps[0])
        pre = pre + product(wide[pl.ds((part + 1) * rows, rows)], taps[1])
        pre = pre + product(wide[pl.ds((part + 2) * rows, rows)], taps[2])
        value = gelu_value(pre)
        branch[here] = value.astype(bf16)
        branches[:, here] = value.T.astype(bf16)
        value = slopes[here] * gelu_slope(pre)
        grad[here] = value.astype(bf16)
        grads[:, here] = value.T.astype(bf16)
    last = started([(grad, stores[1]), (branch, stores[0])], sems, base)
    ends = [(grad.at[pl.ds(3 * rows, rows)], low), (grad.at[pl.ds(0, rows)], high)]
    last += started(ends, sems, base + len(stores))
    width = wide.shape[1] // depth
    if len(outs) == 1:
        for i in range(depth):
            lanes = pl.ds(i * width, width)
            out = outs[0].at[lax.rem(i + depth - z, depth)]
            for k in range(3):
                out[k] = product(grads[...], wide[pl.ds(k * rows, 4 * rows), lanes])
            out[3] = product(branches[...], wide_cot[:, lanes])
        last += started([(outs[0], stores[2])], sems, base + 2)
    else:
        i = 0
        for target, types in roles(depth, z):
            lanes = within(target, width)
            same = outs[i : i + len(types)]
            for k in range(4):
                if k < 3:
                    value = product(
                        grads[...], wide[pl.ds(k * rows, 4 * rows), lanes]
                    )
                else:
                    value = product(branches[...], wide_cot[:, lanes])
                for out in same:
                    out[k] = value.astype(out.dtype)
            i += len(types)
            if depth != 4:
                last += started([(same[0], stores[1 + i])], sems, base + 1 + i)
            elif i == 2:
                last += started([(outs[0], stores[2])], sems, base + 2)
            elif i == 3:
                last += started([(outs[2], stores[3])], sems, base + 3)
            elif i == 4:
                last += started(
                    [
                        ((z == 2, outs[1], outs[3]), stores[4]),
                        ((z == 1, outs[1], outs[3]), stores[5]),
                    ],
                    sems,
                    base + 4,
                )
            else:
                last += started([(outs[4], stores[6])], sems, base + 6)
    finish(last)


def backward_kernel(depth, *refs):
    count = depth + 3 * (depth == 4)
    pieces = refs[:count]
    low, grad, high = refs[count : count + 3]
    stores = refs[count + 3 : count + 7]
    wide, packed, taps, sems = refs[count + 7 : count + 11]
    outs = refs[count + 11 :]
    _, q = position()
    rows = low.shape[0]
    finish(
        started(
            [
                (low, wide.at[pl.ds(0, rows)]),
                (grad, wide.at[pl.ds(rows, 4 * rows)]),
                (high, wide.at[pl.ds(5 * rows, rows)]),
            ]
            + tap_pairs(depth, pieces, packed),
            sems,
        )
    )
    unpack(packed, taps)
    last = []
    for m in (1, 3, 2, 0):
        part = toggled(q, m)
        total = None
        for k in range(3):
            term = transposed_product(wide[within(part + 2 - k, rows)], taps[k])
            total = term if total is None else total + term
        outs[m][...] = total.astype(outs[m].dtype)
        last += started([(outs[m], stores[m])], sems, count + 3 + m)
    finish(last)


def final_kernel(*refs):
    parts = refs[:4]
    dilated, point, held = refs[4:]
    _, q = position()
    quarter = parts[0].shape[1]
    for m in range(4):
        held[m] = parts[m][...].astype(f32)
    for j in range(4):
        m = lax.rem(q + j, 2) + 2 * lax.rem(q // 2 + j // 2, 2)
        here = pl.ds(j * quarter, quarter)
        for k in range(3):
            dilated[k, :, here] = held[m, k].T
        point[:, here] = held[m, 3].T


def call(kernel, outs, args, specs, scratch, flops, limit, kept=pltpu.VMEM):
    nbytes = sum(a.size * a.dtype.itemsize for a in args) + sum(
        math.prod(s) * jnp.dtype(t).itemsize for s, t in outs
    )
    return pl.pallas_call(
        kernel,
        out_shape=[jax.ShapeDtypeStruct(s, t) for s, t in outs],
        in_specs=[pl.BlockSpec(memory_space=m) for m in specs],
        out_specs=[pl.BlockSpec(memory_space=kept)] * len(outs),
        scratch_shapes=scratch,
        compiler_params=pltpu.CompilerParams(vmem_limit_bytes=limit * MIB),
        cost_estimate=pl.CostEstimate(
            flops=flops, bytes_accessed=nbytes, transcendentals=0
        ),
    )(*args)


def local(inputs, norm_gain, dilated_weight, point_weight, cotangent):
    size = lax.axis_size("seq")
    depth = size // 4
    z, q = position()
    core = q % 2
    y = q // 2
    rows, channels = inputs.shape
    own = dilated_weight.shape[1]
    hidden = dilated_weight.shape[2]
    quarter = hidden // 4
    flops = 8 * rows * channels * quarter

    def send(value, target):
        pairs = [(i, target(i)) for i in range(size)]
        return lax.ppermute(
            value, "seq", [p for p in pairs if p[1] is not None and 0 <= p[1] < size]
        )

    def cross(value, m):
        return send(value, lambda i: i ^ m)

    def to_z(value, by):
        return send(value, lambda i: (i + 4 * by) % size)

    def cut(value, start, length, axis):
        return lax.dynamic_slice_in_dim(value, start, length, axis)

    def in_order(first, mine, other, axis):
        return jnp.where(
            first,
            jnp.concatenate([mine, other], axis),
            jnp.concatenate([other, mine], axis),
        )

    quarters = [
        cut(dilated_weight, toggled(q, m) * quarter, quarter, 2) for m in range(4)
    ]
    inputs = after(inputs, *quarters[1:])
    cotangent = after(cotangent, *quarters[1:])
    got = [quarters[0]] + [cross(quarters[m], m) for m in range(1, 4)]
    if own % 16 == 0:
        same = jnp.concatenate(got[:2], 2)
        other = jnp.concatenate(got[2:], 2)
        start_piece = jnp.stack([same, other], 1)
    else:
        same = in_order(core == 0, got[0], got[1], 2)
        other = in_order(core == 0, got[2], got[3], 2)
        start_piece = in_order(y == 0, same[:, None], other[:, None], 1)

    def line(value, pairs):
        return lax.ppermute(
            value,
            "seq",
            [(4 * a + i, 4 * b + i) for a, b in pairs for i in range(4)],
        )

    if depth == 4:
        ups, downs = [start_piece], [start_piece]
        for j in range(3):
            ups.append(line(ups[-1], [(a, a + 1) for a in range(j, 3)]))
            downs.append(line(downs[-1], [(a + 1, a) for a in range(3 - j)]))
        pieces = ups + downs[1:]
    else:
        pieces = [start_piece] + [to_z(start_piece, d) for d in range(1, depth)]

    xfull = inputs.astype(f32)
    ratio = lax.rsqrt(jnp.mean(xfull * xfull, axis=-1, keepdims=True) + 1e-06)
    normed = xfull * ratio * norm_gain
    act = gelu_value(normed).astype(bf16)
    act_late = after(act, got[1])
    cot_late = after(cotangent, start_piece)
    act_across = cross(act_late, 2)
    if depth == 4:
        act_across, pieces[1], pieces[4] = lax.optimization_barrier(
            (act_across, pieces[1], pieces[4])
        )
    edge = send(
        jnp.where(core == y, act_late, act_across),
        lambda i: i + 4 if i % 2 else i - 4,
    )
    edge_other = cross(edge, 1)
    cot_across = cross(after(cot_late, act_across), 2)
    acts = [act_late, cross(act_late, 1), act_across, cross(act_across, 1)]
    cots = [cot_late, cross(cot_late, 1), cot_across, cross(cot_across, 1)]
    point_rows = cut(point_weight, q * quarter, quarter, 0)

    width = channels // depth
    apart = width % 128 == 0
    outs = [
        ((4, quarter, width), t) for _, types in roles(depth, z) for t in types
    ]
    if not apart:
        outs = [((depth, 4, quarter, width), f32)]
    weight_outs = [((4 * rows, quarter), bf16)] * 2 + outs
    *terms, low, high = call(
        functools.partial(weight_kernel, depth),
        weight_outs + [((rows, quarter), bf16)] * 2,
        [*pieces, *acts, edge, edge_other, *cots, point_rows],
        [pltpu.HBM] * (len(pieces) + 10) + [pltpu.VMEM],
        [
            pltpu.VMEM((6 * rows, channels), bf16),
            pltpu.VMEM((4 * rows, channels), bf16),
            pltpu.VMEM((3, depth, 2, own, 2 * quarter), bf16),
            pltpu.VMEM((3, channels, quarter), bf16),
            pltpu.VMEM((quarter, 4 * rows), bf16),
            pltpu.VMEM((quarter, 4 * rows), bf16),
            pltpu.VMEM((4 * rows, quarter), f32),
            pltpu.SemaphoreType.DMA((len(pieces) + 12 + len(weight_outs),)),
            *[pltpu.VMEM(*out) for out in weight_outs],
        ],
        8 * flops,
        60,
        pltpu.HBM,
    )
    branch, pre_grad, *terms = terms
    if not apart:
        terms = [terms[0][d].astype(bf16) for d in range(1, depth)] + [terms[0][0]]
    if depth == 4:
        far, two, up, down, total = terms
        far = line(far, [(0, 1), (3, 2)])
        joined = (two + far.astype(f32)).astype(bf16)
        near_up = line(joined, [(0, 1), (1, 2)])
        near_down = line(joined, [(3, 2), (2, 1)])
        up = up + near_up.astype(f32)
        down = down + near_down.astype(f32)
        parts = [
            line(up.astype(bf16), [(0, 1), (1, 2), (2, 3)]),
            line(down.astype(bf16), [(1, 0), (2, 1), (3, 2)]),
        ]
    else:
        total = terms[-1]
        parts = [to_z(term, d + 1) for d, term in enumerate(terms[:-1])]

    grad_low = send(low, lambda i: i + 4)
    grad_high = send(high, lambda i: i - 4)
    share_outs = [((rows, channels), t) for t in (f32, bf16, f32, bf16)]
    shares = call(
        functools.partial(backward_kernel, depth),
        share_outs,
        [*pieces, grad_low, pre_grad, grad_high],
        [pltpu.HBM] * (len(pieces) + 3),
        [
            pltpu.VMEM((6 * rows, quarter), bf16),
            pltpu.VMEM((3, depth, 2, own, 2 * quarter), bf16),
            pltpu.VMEM((3, channels, quarter), bf16),
            pltpu.SemaphoreType.DMA((len(pieces) + 7,)),
            *[pltpu.VMEM(*out) for out in share_outs],
        ],
        3 * flops,
        60,
        pltpu.HBM,
    )
    away = (shares[2] + cross(shares[3], 1).astype(f32)).astype(bf16)
    arrived = cross(away, 2)

    mine = shares[0] + cross(shares[1], 1).astype(f32)
    act_grad = mine + arrived.astype(f32)
    scaled = act_grad * gelu_slope(normed) * norm_gain
    inner = jnp.mean(scaled * xfull, axis=-1, keepdims=True)
    input_grad = (
        cotangent.astype(f32) + ratio * scaled - xfull * ratio * ratio * ratio * inner
    ).astype(bf16)

    branch = branch.reshape(2, 2, rows, quarter)
    keep = cut(branch, core, 1, 1)[:, 0]
    chip = in_order(core == 0, keep, cross(cut(branch, 1 - core, 1, 1)[:, 0], 1), 2)
    keep = cut(chip, y, 1, 0)[0]
    full = in_order(y == 0, keep, cross(cut(chip, 1 - y, 1, 0)[0], 2), 1)
    outputs = (xfull + product(full, point_weight)).astype(bf16)

    for part in parts:
        total = total + part.astype(f32)
    slices = [cut(total, toggled(q, m) * own, own, 2) for m in range(4)]
    slices = slices[:1] + [cross(slices[m].astype(bf16), m) for m in range(1, 4)]
    slices[3] = after(slices[3], input_grad, outputs)
    dilated_grad, point_grad = call(
        final_kernel,
        [((3, own, hidden), f32), ((own, hidden), f32)],
        slices,
        [pltpu.VMEM] * 4,
        [pltpu.VMEM((4, 4, quarter, own), f32)],
        1024,
        16,
    )
    return (outputs, input_grad, dilated_grad, point_grad.T)


def solution(mesh):
    placed = (
        P(("groups", "seq"), None),
        P(),
        P(None, "seq", None),
        P(),
        P(("groups", "seq"), None),
    )
    return jax.shard_map(
        local,
        mesh=mesh,
        in_specs=placed,
        out_specs=(
            P(("groups", "seq"), None),
            P(("groups", "seq"), None),
            P("groups", "seq", None),
            P("groups", "seq"),
        ),
        check_vma=False,
    )
```
